32 devices in a mesh: dp: 16 (over z, x, core), expert: 2 (over y).
Axes of the slice: x: 2, y: 2, z: 4, core: 2. Of those that a mesh axis runs over, the one named last changes fastest.
Arguments:
- grad_out: bfloat16 [16384, 3072], P(('dp', 'expert')), may hold values from -0.19921875 to 0.19921875
- expert_ids: int32 [16384, 2], P(('dp', 'expert')), may hold values from 0 to 7, all different within a row; in each aligned block of 512 rows (0 to 511, 512 to 1023, ...) at most 192 rows name the same one
- gate_probs: float32 [16384, 2], P(('dp', 'expert')), may hold values from 0.1 to 1
- saved_gate: bfloat16 [6144, 2, 1024], P('dp', 'expert'), may hold values from -6 to 6
- saved_up: bfloat16 [6144, 2, 1024], P('dp', 'expert'), may hold values from -6 to 6
- master: float32 [2, 1024, 3072], P('expert', 'dp')
- moment_one: float32 [2, 1024, 3072], P('expert', 'dp'), may hold values from -2 to 2
- moment_two: float32 [2, 1024, 3072], P('expert', 'dp'), may hold values from 0.05 to 1
Outputs:
- new_master: float32 [2, 1024, 3072], P('expert', 'dp')
- new_moment_one: float32 [2, 1024, 3072], P('expert', 'dp')
- new_moment_two: float32 [2, 1024, 3072], P('expert', 'dp')
- new_weights: float32 [2, 1024, 3072], P('expert')
The draws below stay inside these ranges and needn't reach their ends.
Inputs may be any that keep to these rules, and one draw needn't show every extreme that they name: `expert_ids`: in each aligned block of 512 rows (the tokens of one device) no expert is named by more than 192 rows, a bound that some block reaches.
All inputs are finite; a program needn't handle non-finite values.
Results may differ from the reference program's by a relative error of at most 0.00035.
Values may be sent and summed in bfloat16 or wider, within the bound.
No kernel may reach another device: no remote copies, remote signals or barrier semaphores. Data moves between devices by JAX's collectives and lax.ppermute only.
A program may use at most 128 MiB of HBM per device.

```python
import math
import jax
import jax.numpy as jnp
import numpy as np
from jax import lax

D = 3072
EXPERTS_ALL = 8
HID_DEV = 1024
TOK_DEV = 512
BLOCKS = 2
CAP = 192
TOKENS = 16384
SLOTS = 6144


def draw_master(key, part):
    key_rows, key_cols, key_base = jax.random.split(key, 3)
    rows = jnp.exp(jax.random.uniform(key_rows, (BLOCKS, HID_DEV, 1), jnp.float32) * math.log(10.0))
    cols = jnp.exp(jax.random.uniform(key_cols, (1, 1, D), jnp.float32) * math.log(10.0))
    base = jax.random.normal(key_base, (BLOCKS, HID_DEV, D), jnp.float32)
    return (0.02 * rows * cols * base).astype(jnp.float32)


def block_levels(key, shape, pieces, low, top_value):
    def one(dim, parts):
        steps = jax.random.uniform(jax.random.fold_in(jax.random.fold_in(key, 6), dim), (parts,), jnp.float32, low / len(pieces), top_value / len(pieces))
        return jnp.repeat(jnp.exp(steps), shape[dim] // parts).reshape((-1,) + (1,) * (len(shape) - dim - 1))

    level = one(*pieces[0])
    for cut in pieces[1:]:
        level = level * one(*cut)
    return level


def routed_block(stream_key, own, number, rows, amount, top, limit, skew):
    order = jax.random.permutation(stream_key, amount)
    packed, usual = load_shares(amount, rows * top, limit, skew, True), load_shares(amount, rows * top, limit, skew, False)
    places = jnp.arange(amount)

    def named(tallies, turn):
        used = int((tallies > 0).sum())
        fixed = max(1, used // 4)
        passed = fixed + (places - fixed + turn * (used - fixed)) % max(1, amount - fixed)
        return jnp.zeros((amount,), jnp.int32).at[order[jnp.where(places < fixed, places, passed)]].set(jnp.asarray(tallies, jnp.int32))

    tallies = jnp.where(number % 4 == 0, named(packed, number // 4), named(usual, number - number // 4 - 1))
    mixed = jax.random.permutation(jax.random.fold_in(own, 3), amount)
    giver, sink = mixed[0:amount // 2 * 2:2], mixed[1:amount // 2 * 2:2]
    slack = jnp.minimum(tallies[giver] - 1, limit - tallies[sink]) // 2
    slack = jnp.where((giver == order[0]) | (sink == order[0]) | (tallies[sink] == 0), 0, jnp.maximum(slack, 0))
    passed = jax.random.randint(jax.random.fold_in(own, 4), (amount // 2,), 0, 1 << 20) % (slack + 1)
    tallies = tallies.at[giver].add(-passed).at[sink].add(passed)
    members = jnp.searchsorted(jnp.cumsum(tallies), jnp.arange(rows * top), side="right").astype(jnp.int32)
    grid = members.reshape(top, rows).T
    grid = grid[jax.random.permutation(jax.random.fold_in(own, 1), rows)]
    turn = jax.random.randint(jax.random.fold_in(own, 2), (rows, 1), 0, top)
    return jnp.take_along_axis(grid, (jnp.arange(top)[None, :] + turn) % top, axis=1)


def load_shares(count, total, limit, slope, full):
    loads = [(1 << 20) // math.isqrt(grade ** slope) + 1 for grade in range(1, count + 1)]
    largest = limit if full else min(limit, max(-(-total // count), total * loads[0] // sum(loads)))
    least = 1 if total - largest >= count - 1 else 0
    holding, rest = [largest] + [least] * (count - 1), total - largest - least * (count - 1)
    while rest > 0:
        candidates = [i for i in range(1, count) if holding[i] < largest] or [i for i in range(1, count) if holding[i] < limit]
        whole, budget = sum([loads[i] for i in candidates]), rest
        for i in candidates:
            extra = min(limit - holding[i], max(1, budget * loads[i] // whole), rest)
            holding[i] = holding[i] + extra
            rest = rest - extra
    return np.array(holding)


def centred(key, extent, scale, most, shards=(), kind=jnp.bfloat16):
    drawn = scale * jax.random.normal(key, extent, jnp.float32)
    if shards:
        drawn = drawn * block_levels(key, extent, shards, -0.22, 0.18)
    return jnp.clip(drawn, -most, most).astype(kind)


def setup_inputs(seed: int = 0) -> dict:
    key_list = jax.random.split(jax.random.key(seed), 9)
    grad_out = centred(key_list[0], (TOKENS, D), 0.03, 0.19921875, ((0, 32),))
    expert_ids_keys = jax.random.split(jax.random.fold_in(key_list[1], 1), TOKENS // TOK_DEV)
    expert_ids_turns = jax.random.permutation(jax.random.fold_in(key_list[1], 3), TOKENS // TOK_DEV)
    expert_ids = jax.vmap(lambda own, number: routed_block(jax.random.fold_in(key_list[1], 2), own, number, TOK_DEV, EXPERTS_ALL, 2, CAP, 2))(expert_ids_keys, expert_ids_turns).reshape((TOKENS, 2))
    gate_probs = jnp.clip(0.1 + 0.9 * jax.random.uniform(key_list[2], (TOKENS, 2), jnp.float32) ** block_levels(key_list[2], (TOKENS, 2), ((0, 32),), -0.2, 0.2), 0.1, 1.0)
    saved_gate = centred(key_list[3], (SLOTS, BLOCKS, HID_DEV), 1.0, 6.0, ((0, 16), (1, 2)))
    saved_up = centred(key_list[4], (SLOTS, BLOCKS, HID_DEV), 1.0, 6.0, ((0, 16), (1, 2)))
    master = draw_master(jax.random.fold_in(key_list[8], 71), 0)
    moment_one = centred(key_list[6], (BLOCKS, HID_DEV, D), 0.3, 2.0, ((0, 2), (1, 16)), jnp.float32)
    moment_two = jnp.clip(jnp.exp(math.log(1.0) - 2.9957323 * jax.random.uniform(key_list[7], (BLOCKS, HID_DEV, D), jnp.float32) ** block_levels(key_list[7], (BLOCKS, HID_DEV, D), ((0, 2), (1, 16)), -0.2, 0.2)), 0.05, 1.0)
    return dict(grad_out=grad_out, expert_ids=expert_ids, gate_probs=gate_probs, saved_gate=saved_gate, saved_up=saved_up, master=master, moment_one=moment_one, moment_two=moment_two)


def block_grad(pair, dispatched):
    gate_part, up_part = pair
    hidden = (jax.nn.silu(gate_part.astype(jnp.float32)) * up_part.astype(jnp.float32)).astype(jnp.bfloat16)
    return jnp.dot(hidden.T, dispatched, preferred_element_type=jnp.float32)

def reference(grad_out, expert_ids, gate_probs, saved_gate, saved_up, master, moment_one, moment_two):
    groups = TOKENS // TOK_DEV
    ids = expert_ids.reshape(groups, TOK_DEV, 2)
    probs = gate_probs.reshape(groups, TOK_DEV, 2)
    hit = ids == 0
    chosen = jnp.any(hit, axis=2)
    weight = lax.optimization_barrier(jnp.sum(jnp.where(hit, probs, jnp.float32(0.0)), axis=2))
    slot = jnp.cumsum(chosen.astype(jnp.int32), axis=1).astype(jnp.int32) - 1
    scaled = (weight[:, :, None] * grad_out.reshape(groups, TOK_DEV, D).astype(jnp.float32)).astype(jnp.bfloat16)
    places = jnp.arange(CAP, dtype=jnp.int32)
    placing = ((slot[:, None, :] == places[None, :, None]) & chosen[:, None, :]).astype(jnp.float32)
    dispatched = jnp.einsum('bct,btd->bcd', placing, scaled.astype(jnp.float32)).astype(jnp.bfloat16)
    dispatched = dispatched.reshape(groups * CAP, D)
    gates = jnp.moveaxis(saved_gate, 1, 0)
    ups = jnp.moveaxis(saved_up, 1, 0)
    grad = lax.map(lambda pair: block_grad(pair, dispatched), (gates, ups))
    new_one = 0.9 * moment_one + 0.1 * grad
    new_two = 0.95 * moment_two + 0.05 * grad * grad
    step = new_one / (1.0 - 0.9 ** 20) / (jnp.sqrt(new_two / (1.0 - 0.95 ** 20)) + 1e-08)
    wrms = jnp.sqrt(lax.optimization_barrier(jnp.mean(master * master, axis=-1, keepdims=True)) + 1e-06)
    srms = jnp.sqrt(lax.optimization_barrier(jnp.mean(step * step, axis=-1, keepdims=True)) + 1e-06)
    factor = jnp.minimum(1.0, 0.02 * wrms / (0.01 * srms))
    new_master = master - 0.01 * factor * step
    return (new_master, new_one, new_two, new_master)
```

```python
import jax
import jax.numpy as jnp
from jax import lax
from jax.sharding import PartitionSpec as P

F16 = jnp.float16
F32 = jnp.float32
BF16 = jnp.bfloat16
CHUNKS = 4


def build(mesh):
    devices = mesh.shape["dp"]
    experts = mesh.shape["expert"]
    rows_a = 4
    rows_b = devices // (2 * rows_a)

    def place(a, b, c):
        return ((a % rows_a) * rows_b + b % rows_b) * 2 + c % 2

    spots = [(a, b, c) for a in range(rows_a) for b in range(rows_b) for c in range(2)]

    def shift_a(value, k):
        return lax.ppermute(value, "dp", [(place(a, b, c), place(a + k, b, c)) for a, b, c in spots])

    def shift_b(value, k):
        return lax.ppermute(value, "dp", [(place(a, b, c), place(a, b + k, c)) for a, b, c in spots])

    def swap_core(value):
        return lax.ppermute(value, "dp", [(place(a, b, c), place(a, b, c + 1)) for a, b, c in spots])

    def shift_expert(value, k):
        return lax.ppermute(value, "expert", [(e, (e + k) % experts) for e in range(experts)])

    def local(grad_out, expert_ids, gate_probs, saved_gate, saved_up, master, moment_one, moment_two):
        me = lax.axis_index("dp")
        core = me % 2
        at_b = (me // 2) % rows_b
        at_a = me // (2 * rows_b)
        at_e = lax.axis_index("expert")
        tok_rows, dim = grad_out.shape
        cap_rows = tok_rows * 3 // 8
        own = master.shape[1]
        slot_rows, _, width = saved_gate.shape

        hit = expert_ids == 0
        chosen = jnp.any(hit, axis=1)
        weight = jnp.sum(jnp.where(hit, gate_probs, jnp.float32(0.0)), axis=1)
        slot = jnp.cumsum(chosen.astype(jnp.int32)) - 1
        scaled = (weight[:, None] * grad_out.astype(F32)).astype(BF16)
        places = jnp.arange(cap_rows, dtype=jnp.int32)
        placing = ((slot[None, :] == places[:, None]) & chosen[None, :]).astype(BF16)
        dispatched = jnp.dot(placing, scaled, preferred_element_type=F32).astype(BF16)

        def rolled(saved):
            saved = saved.reshape(experts, cap_rows, width)
            parts = [lax.dynamic_index_in_dim(saved, (at_e + j) % experts, 0, False) for j in range(experts)]
            return jnp.concatenate(parts, axis=0).astype(F32)

        hidden = (jax.nn.silu(rolled(saved_gate)) * rolled(saved_up)).astype(BF16)
        hidden = hidden.T.reshape(rows_a, rows_b, 2, own, slot_rows).transpose(2, 1, 0, 3, 4)
        hidden_mine = lax.dynamic_index_in_dim(hidden, core, 0, False)
        hidden_other = swap_core(lax.dynamic_index_in_dim(hidden, 1 - core, 0, False))
        hidden_all = jnp.concatenate([hidden_mine, hidden_other], axis=-1)
        blocks = [
            lax.dynamic_index_in_dim(hidden_all, (at_b + k) % rows_b, 0, False).reshape(rows_a * own, 2 * slot_rows)
            for k in range(rows_b)
        ]

        bound = jnp.max(jnp.abs(master[0]), axis=-1, keepdims=True) + 0.08
        bounds = lax.all_gather(bound, "dp", axis=0, tiled=True)

        largest = 2 * rows_b * slot_rows * 36.0 * 0.2
        shrink = 1.0
        while largest * shrink > 60000.0:
            shrink *= 0.5

        size = dim // CHUNKS
        grads = []
        for i in range(CHUNKS):
            part = dispatched[:, i * size : (i + 1) * size]
            parts = [part] + [shift_expert(part, -j) for j in range(1, experts)]
            mine = jnp.concatenate(parts, axis=0)
            both = jnp.concatenate([mine, swap_core(mine)], axis=0)
            total = jnp.dot(blocks[0], both, preferred_element_type=F32) * shrink
            for k in range(1, rows_b):
                send = (jnp.dot(blocks[k], both, preferred_element_type=F32) * shrink).astype(F16)
                total = total + shift_b(send, k).astype(F32)
            total = total.reshape(rows_a, own, size)
            grad = lax.dynamic_index_in_dim(total, at_a, 0, False)
            for k in range(1, rows_a):
                send = lax.dynamic_index_in_dim(total, (at_a + k) % rows_a, 0, False).astype(F16)
                grad = grad + shift_a(send, k).astype(F32)
            grads.append(grad)
        grad = (jnp.concatenate(grads, axis=1) * (1.0 / shrink)).reshape(master.shape)

        new_one = 0.9 * moment_one + 0.1 * grad
        new_two = 0.95 * moment_two + 0.05 * grad * grad
        step = new_one / (1.0 - 0.9**20) / (jnp.sqrt(new_two / (1.0 - 0.95**20)) + 1e-08)
        wrms = jnp.sqrt(jnp.mean(master * master, axis=-1, keepdims=True) + 1e-06)
        srms = jnp.sqrt(jnp.mean(step * step, axis=-1, keepdims=True) + 1e-06)
        factor = jnp.minimum(1.0, 0.02 * wrms / (0.01 * srms))
        new_master = master - 0.01 * factor * step

        weights = jnp.zeros((width, dim), F32)

        def put(weights, coded, a, b, c):
            row = place(a, b, c) * own
            scale = lax.dynamic_slice(bounds, (row, 0), (own, 1)) * (1.0 / 32768.0)
            return lax.dynamic_update_slice(weights, coded.astype(F32) * scale, (row, 0))

        coded = (new_master[0] * (32768.0 / bound)).astype(F16)
        for i in range(rows_a):
            for j in range(rows_b):
                held = coded if j == 0 else shift_b(coded, j)
                weights = put(weights, held, at_a - i, at_b - j, core)
                weights = put(weights, swap_core(held), at_a - i, at_b - j, 1 - core)
            if i < rows_a - 1:
                coded = shift_a(coded, 1)
        return (new_master, new_one, new_two, weights[None])

    return local


def solution(mesh):
    return jax.shard_map(
        build(mesh),
        mesh=mesh,
        in_specs=(
            P(("dp", "expert"), None),
            P(("dp", "expert"), None),
            P(("dp", "expert"), None),
            P("dp", "expert", None),
            P("dp", "expert", None),
            P("expert", "dp", None),
            P("expert", "dp", None),
            P("expert", "dp", None),
        ),
        out_specs=(
            P("expert", "dp", None),
            P("expert", "dp", None),
            P("expert", "dp", None),
            P("expert", None, None),
        ),
        check_vma=False,
    )
```

```python
import functools

import jax
import jax.numpy as jnp
from jax import lax
from jax.experimental import pallas as pl
from jax.experimental.pallas import tpu as pltpu
from jax.sharding import PartitionSpec as P

F16 = jnp.float16
F32 = jnp.float32
BF16 = jnp.bfloat16
CHUNKS = (768, 768, 768, 768)
STREAMS = (3072,)
PUT_FLOPS = 2 << 30


def after(value, other):
    return lax.optimization_barrier((value, other))[0]


def dispatch_kernel(cap_rows, ids, probs, grad, *outs):
    tok_rows = ids.shape[1]
    hit = ids[...] == 0
    weight = jnp.sum(jnp.where(hit, probs[...], 0.0), axis=0, keepdims=True)
    chosen = jnp.sum(jnp.where(hit, 1.0, 0.0), axis=0, keepdims=True)
    earlier = lax.broadcasted_iota(jnp.int32, (tok_rows, tok_rows), 0) < lax.broadcasted_iota(
        jnp.int32, (tok_rows, tok_rows), 1
    )
    slot = jnp.dot(
        jnp.broadcast_to(chosen, (8, tok_rows)).astype(BF16),
        jnp.where(earlier, 1.0, 0.0).astype(BF16),
        preferred_element_type=F32,
    )[:1]
    slot = jnp.where(chosen > 0.0, slot, -1.0)
    places = lax.broadcasted_iota(jnp.int32, (cap_rows, tok_rows), 0).astype(F32)
    placing = jnp.where(slot == places, 1.0, 0.0).astype(BF16)
    weight = jnp.broadcast_to(weight, (128, tok_rows)).T[:, :1]
    first = 0
    for out in outs:
        size = out.shape[1]
        scaled = (weight * grad[:, first : first + size].astype(F32)).astype(BF16)
        out[...] = jnp.dot(placing, scaled, preferred_element_type=F32).astype(BF16)
        first += size


def dispatch(ids, probs, grad, cap_rows):
    vmem = pl.BlockSpec(memory_space=pltpu.VMEM)
    return pl.pallas_call(
        functools.partial(dispatch_kernel, cap_rows),
        out_shape=tuple(jax.ShapeDtypeStruct((cap_rows, size), BF16) for size in CHUNKS),
        in_specs=[vmem] * 3,
        out_specs=(vmem,) * len(CHUNKS),
        compiler_params=pltpu.CompilerParams(vmem_limit_bytes=16 << 20),
        name="dispatch",
    )(ids.T, probs.T, grad)


def put_kernel(marks, aliased, starts, *refs):
    refs = refs[1:] if aliased else refs
    pieces, out, sems = refs[: len(marks)], refs[len(marks)], refs[len(marks) + 1]
    copies = []
    for n, (index, column) in enumerate(marks):
        height, size = pieces[n].shape
        row = pl.multiple_of(starts[index], height)
        spot = out.at[pl.ds(row, height), pl.ds(column, size)]
        copies.append(pltpu.make_async_copy(pieces[n], spot, sems.at[n]))
        copies[-1].start()
    for copy in copies:
        copy.wait()


def put(weights, shape, starts, marks, pieces):
    aliased = weights is not None
    spec = pl.BlockSpec(memory_space=pl.ANY)
    return pl.pallas_call(
        functools.partial(put_kernel, tuple(marks), aliased),
        out_shape=jax.ShapeDtypeStruct(shape, F32),
        in_specs=[pl.BlockSpec(memory_space=pltpu.SMEM)] + [spec] * (aliased + len(pieces)),
        out_specs=spec,
        scratch_shapes=[pltpu.SemaphoreType.DMA((len(pieces),))],
        input_output_aliases={1: 0} if aliased else {},
        compiler_params=pltpu.CompilerParams(vmem_limit_bytes=1 << 20),
        cost_estimate=pl.CostEstimate(flops=PUT_FLOPS, bytes_accessed=0, transcendentals=0),
        name="put",
    )(starts, *([weights] if aliased else []), *pieces)


def hidden_kernel(sizes, at, gate, up, mine, send):
    experts, rows_b, rows_a, own = sizes
    cap_rows = gate.shape[0] // experts
    at_e, at_b, core = at[0], at[1], at[2]
    values = []
    for j in range(experts):
        spot = pl.ds(pl.multiple_of(lax.rem(at_e + j, experts) * cap_rows, cap_rows), cap_rows)
        value = gate[spot, :].astype(F32)
        values.append(value / (1.0 + jnp.exp(-value)) * up[spot, :].astype(F32))
    value = jnp.concatenate(values, axis=0).T.astype(BF16)
    for b in range(rows_b):
        k = lax.rem(b - at_b + rows_b, rows_b)
        for a in range(rows_a):
            first = (a * rows_b + b) * 2 * own
            low, high = value[first : first + own], value[first + own : first + 2 * own]
            rows = pl.ds(a * own, own)
            mine[k, rows, :] = jnp.where(core == 0, low, high)
            send[k, rows, :] = jnp.where(core == 0, high, low)


def hidden_pieces(at, gate, up, sizes):
    experts, rows_b, rows_a, own = sizes
    shape = jax.ShapeDtypeStruct((rows_b, rows_a * own, gate.shape[0]), BF16)
    vmem = pl.BlockSpec(memory_space=pltpu.VMEM)
    return pl.pallas_call(
        functools.partial(hidden_kernel, sizes),
        out_shape=(shape, shape),
        in_specs=[pl.BlockSpec(memory_space=pltpu.SMEM), vmem, vmem],
        out_specs=(vmem, vmem),
        compiler_params=pltpu.CompilerParams(vmem_limit_bytes=(8 << 20) * max(1, experts // 2)),
        name="hidden_pieces",
    )(at, gate, up)


def product_kernel(scale, left, *refs):
    pieces, kept, sent, rows = refs[:-3], refs[-3], refs[-2], refs[-1]
    height = pieces[0].shape[0]
    for n, piece in enumerate(pieces):
        rows[n * height : (n + 1) * height, :] = piece[...]
    for k in range(left.shape[0]):
        total = jnp.dot(left[k], rows[...], preferred_element_type=F32)
        total = total * scale if scale != 1.0 else total
        if k == 0:
            kept[...] = total
        else:
            sent[k - 1] = total


def product(left, pieces, scale):
    count, half, depth = left.shape
    size = pieces[0].shape[1]
    vmem = pl.BlockSpec(memory_space=pltpu.VMEM)
    return pl.pallas_call(
        functools.partial(product_kernel, scale),
        out_shape=(
            jax.ShapeDtypeStruct((half, size), F32),
            jax.ShapeDtypeStruct((count - 1, half, size), F32),
        ),
        in_specs=[vmem] * (1 + len(pieces)),
        out_specs=(vmem, vmem),
        scratch_shapes=[pltpu.VMEM((depth, size), BF16)],
        compiler_params=pltpu.CompilerParams(vmem_limit_bytes=16 << 20),
        cost_estimate=pl.CostEstimate(flops=2 * count * half * depth * size, bytes_accessed=0, transcendentals=0),
        name="product",
    )(left, *pieces)


def build(mesh):
    devices = mesh.shape["dp"]
    experts = mesh.shape["expert"]
    rows_a = 4
    rows_b = devices // (2 * rows_a)

    def place(a, b, c):
        return ((a % rows_a) * rows_b + b % rows_b) * 2 + c % 2

    spots = [(a, b, c) for a in range(rows_a) for b in range(rows_b) for c in range(2)]

    def flip_a(value, k):
        return lax.ppermute(value, "dp", [(place(a, b, c), place(a ^ k, b, c)) for a, b, c in spots])

    ring = [p ^ (p >> 1) for p in range(rows_a)]

    def step_ring(value):
        pairs = [(p, (p + 1) % rows_a) for p in range(rows_a)]
        return lax.ppermute(
            value,
            "dp",
            [(place(ring[p], b, c), place(ring[q], b, c)) for p, q in pairs for b in range(rows_b) for c in range(2)],
        )

    def shift_b(value, k):
        return lax.ppermute(value, "dp", [(place(a, b, c), place(a, b + k, c)) for a, b, c in spots])

    def swap_core(value):
        return lax.ppermute(value, "dp", [(place(a, b, c), place(a, b, c + 1)) for a, b, c in spots])

    def shift_expert(value, k):
        return lax.ppermute(value, "expert", [(e, (e + k) % experts) for e in range(experts)])

    def local(grad_out, expert_ids, gate_probs, saved_gate, saved_up, master, moment_one, moment_two):
        me = lax.axis_index("dp")
        core = me % 2
        at_b = (me // 2) % rows_b
        at_a = me // (2 * rows_b)
        at_e = lax.axis_index("expert")
        tok_rows, dim = grad_out.shape
        cap_rows = tok_rows * 3 // 8
        own = master.shape[1]
        slot_rows, _, width = saved_gate.shape

        count = len(CHUNKS)
        cuts = [sum(CHUNKS[:i]) for i in range(count)]
        parts = dispatch(expert_ids, gate_probs, grad_out, cap_rows)

        hidden_mine, hidden_send = hidden_pieces(
            jnp.stack([at_e, at_b, core]).astype(jnp.int32),
            saved_gate.reshape(slot_rows, width),
            saved_up.reshape(slot_rows, width),
            (experts, rows_b, rows_a, own),
        )
        hidden_other = swap_core(hidden_send)
        left = jnp.concatenate([hidden_mine, hidden_other], axis=2)

        largest = 2 * rows_b * slot_rows * 36.0 * 0.2
        shrink = 1.0
        while largest * shrink > 60000.0:
            shrink *= 0.5

        far = []
        for i in range(count):
            part = parts[i]
            if i == 1:
                part = after(part, hidden_send)
            elif i > 1:
                part = after(part, far[i - 2][-1])
            far.append([shift_expert(part, -j) for j in range(1, experts)])
        kept, sent = [], []
        for i in range(count):
            here = [parts[i]] + (far[i] if i == 0 else [after(x, sent[i - 1][-1]) for x in far[i]])
            there = [swap_core(x) for x in here]
            mine, others = product(left, here + there, shrink)
            kept.append(mine)
            sent.append([others[k].astype(F16) for k in range(rows_b - 1)])
        got = [[shift_b(x, k + 1) for k, x in enumerate(xs)] for xs in sent]
        halves = []
        for i in range(count):
            total = kept[i]
            for x in got[i]:
                total = total + (after(x, sent[i + 1][-1]) if i + 1 < count else x).astype(F32)
            total = total.reshape(rows_a // 2, 2, own, CHUNKS[i])
            mine = lax.dynamic_index_in_dim(total, at_a % 2, 1, False)
            send = lax.dynamic_index_in_dim(total, 1 - at_a % 2, 1, False).astype(F16)
            halves.append((mine, send))
        quarters = []
        for i in range(count):
            mine, send = halves[i]
            came = flip_a(send, 1)
            total = mine + (after(came, halves[i + 1][1]) if i + 1 < count else came).astype(F32)
            mine = lax.dynamic_index_in_dim(total, at_a // 2, 0, False)
            send = lax.dynamic_index_in_dim(total, 1 - at_a // 2, 0, False).astype(F16)
            quarters.append((mine, send))
        grads = []
        for i in range(count):
            mine, send = quarters[i]
            came = flip_a(send, 2)
            grads.append(mine + (after(came, quarters[i + 1][1]) if i + 1 < count else came).astype(F32))
        grad = (jnp.concatenate(grads, axis=1) * (1.0 / shrink)).reshape(master.shape)

        new_one = 0.9 * moment_one + 0.1 * grad
        new_two = 0.95 * moment_two + 0.05 * grad * grad
        step = new_one / (1.0 - 0.9**20) / (jnp.sqrt(new_two / (1.0 - 0.95**20)) + 1e-08)
        wrms = jnp.sqrt(jnp.mean(master * master, axis=-1, keepdims=True) + 1e-06)
        srms = jnp.sqrt(jnp.mean(step * step, axis=-1, keepdims=True) + 1e-06)
        factor = jnp.minimum(1.0, 0.02 * wrms / (0.01 * srms))
        new_master = master - 0.01 * factor * step

        bound = jnp.max(jnp.abs(master[0]), axis=-1, keepdims=True) + 0.08
        power = jnp.floor(jnp.log2(bound))
        coded = (new_master[0] * jnp.exp2(13.0 - power)).astype(F16)
        coded = jnp.concatenate([coded, jnp.broadcast_to(power.astype(F16), (own, 128))], axis=1)
        pad = coded.shape[1] - dim
        edges = [(sum(STREAMS[:n]), sum(STREAMS[: n + 1])) for n in range(len(STREAMS))]
        coded = jnp.concatenate([coded[:, dim:], coded[:, :dim]], axis=1)
        streams = [coded[:, (low + pad if n else low) : high + pad] for n, (low, high) in enumerate(edges)]
        held = [[value] for value in streams]
        moved = [[[shift_b(value, j) for j in range(1, rows_b)]] for value in streams]
        for value, along in zip(held, moved):
            for i in range(1, rows_a):
                value.append(step_ring(value[-1]))
                along.append([shift_b(value[-1], j) for j in range(1, rows_b)])
        groups = [[(0, 0, n) for n in range(len(STREAMS))]]
        for i in range(1, rows_a + 1):
            for n in range(len(STREAMS)):
                group = [(i, 0, n)] if i < rows_a else []
                groups.append(group + [(i - 1, j, n) for j in range(1, rows_b)])
        scales, weights, late = {}, None, []
        back = (at_a ^ (at_a >> 1)) + rows_a - jnp.arange(rows_a, dtype=jnp.int32)
        from_a = (back % rows_a) ^ (back % rows_a >> 1)
        from_b = (at_b + rows_b - jnp.arange(rows_b, dtype=jnp.int32)) % rows_b
        from_core = (core + jnp.arange(2, dtype=jnp.int32)) % 2
        starts = (from_a[:, None, None] * rows_b + from_b[:, None]) * 2 + from_core
        starts = (starts * own).astype(jnp.int32).reshape(-1)
        for group in groups + [[]]:
            pieces = late
            late = []
            for i, j, n in group:
                value = held[n][i] if j == 0 else moved[n][i][j - 1]
                pieces = pieces + [((i, j, 0), n, value)]
                late.append(((i, j, 1), n, swap_core(value)))
            values = []
            for spot, n, value in pieces:
                if n == 0:
                    scales[spot] = jnp.exp2(value[:, :1].astype(F32) - 13.0)
                    value = value[:, pad:]
                values.append(value.astype(F32) * scales[spot])
            marks = [((i * rows_b + j) * 2 + k, edges[n][0]) for (i, j, k), n, _ in pieces]
            weights = put(weights, (width, dim), starts, marks, values)
        return (new_master, new_one, new_two, weights[None])

    return local


def solution(mesh):
    return jax.shard_map(
        build(mesh),
        mesh=mesh,
        in_specs=(
            P(("dp", "expert"), None),
            P(("dp", "expert"), None),
            P(("dp", "expert"), None),
            P("dp", "expert", None),
            P("dp", "expert", None),
            P("expert", "dp", None),
            P("expert", "dp", None),
            P("expert", "dp", None),
        ),
        out_specs=(
            P("expert", "dp", None),
            P("expert", "dp", None),
            P("expert", "dp", None),
            P("expert", None, None),
        ),
        check_vma=False,
    )
```

```python
import functools

import jax
import jax.numpy as jnp
from jax import lax
from jax.experimental import pallas as pl
from jax.experimental.pallas import tpu as pltpu
from jax.sharding import PartitionSpec as P

F16 = jnp.float16
F32 = jnp.float32
BF16 = jnp.bfloat16
CHUNKS = (1280, 1792)
PUT_FLOPS = 2 << 30
HIDDEN_FLOPS = 8 << 30
OFFSET = 3


def after(value, other):
    return lax.optimization_barrier((value, other))[0]


def dispatch_kernel(cap_rows, ids_in, probs_in, grad_in, *refs):
    outs, (ids, probs, grad, sems) = refs[:-4], refs[-4:]
    cuts = [sum(out.shape[1] for out in outs[:n]) for n in range(len(outs))]
    spots = [pl.ds(first, out.shape[1]) for first, out in zip(cuts, outs)]
    copies = [pltpu.make_async_copy(ids_in, ids, sems.at[0]), pltpu.make_async_copy(probs_in, probs, sems.at[1])]
    copies += [
        pltpu.make_async_copy(grad_in.at[:, spot], grad.at[:, spot], sems.at[2 + n]) for n, spot in enumerate(spots)
    ]
    for copy in copies:
        copy.start()
    copies[0].wait()
    copies[1].wait()
    tok_rows = ids.shape[1]
    hit = ids[...] == 0
    weight = jnp.sum(jnp.where(hit, probs[...], 0.0), axis=0, keepdims=True)
    chosen = jnp.sum(jnp.where(hit, 1.0, 0.0), axis=0, keepdims=True)
    earlier = lax.broadcasted_iota(jnp.int32, (tok_rows, tok_rows), 0) < lax.broadcasted_iota(
        jnp.int32, (tok_rows, tok_rows), 1
    )
    slot = jnp.dot(
        jnp.broadcast_to(chosen, (8, tok_rows)).astype(BF16),
        jnp.where(earlier, 1.0, 0.0).astype(BF16),
        preferred_element_type=F32,
    )[:1]
    slot = jnp.where(chosen > 0.0, slot, -1.0)
    places = lax.broadcasted_iota(jnp.int32, (cap_rows, tok_rows), 0).astype(F32)
    placing = jnp.where(slot == places, 1.0, 0.0).astype(BF16)
    weight = jnp.broadcast_to(weight, (128, tok_rows)).T[:, :1]
    for n, (spot, out) in enumerate(zip(spots, outs)):
        copies[2 + n].wait()
        scaled = (weight * grad[:, spot].astype(F32)).astype(BF16)
        out[...] = jnp.dot(placing, scaled, preferred_element_type=F32).astype(BF16)


def dispatch(ids, probs, grad, cap_rows):
    ids, probs = ids.T, probs.T
    vmem, hbm = pl.BlockSpec(memory_space=pltpu.VMEM), pl.BlockSpec(memory_space=pltpu.HBM)
    return pl.pallas_call(
        functools.partial(dispatch_kernel, cap_rows),
        out_shape=tuple(jax.ShapeDtypeStruct((cap_rows, size), BF16) for size in CHUNKS),
        in_specs=[hbm] * 3,
        out_specs=(vmem,) * len(CHUNKS),
        scratch_shapes=[
            pltpu.VMEM(ids.shape, ids.dtype),
            pltpu.VMEM(probs.shape, probs.dtype),
            pltpu.VMEM(grad.shape, grad.dtype),
            pltpu.SemaphoreType.DMA((2 + len(CHUNKS),)),
        ],
        compiler_params=pltpu.CompilerParams(vmem_limit_bytes=56 << 20),
        name="dispatch",
    )(ids, probs, grad)


def put_kernel(marks, aliased, starts, *refs):
    refs = refs[1:] if aliased else refs
    pieces, out, sems = refs[: len(marks)], refs[len(marks)], refs[len(marks) + 1]
    copies = []
    for n, (index, column) in enumerate(marks):
        height, size = pieces[n].shape
        row = pl.multiple_of(starts[index], height)
        spot = out.at[pl.ds(row, height), pl.ds(column, size)]
        copies.append(pltpu.make_async_copy(pieces[n], spot, sems.at[n]))
        copies[-1].start()
    for copy in copies:
        copy.wait()


def put(weights, shape, starts, marks, pieces):
    aliased = weights is not None
    spec = pl.BlockSpec(memory_space=pl.ANY)
    return pl.pallas_call(
        functools.partial(put_kernel, tuple(marks), aliased),
        out_shape=jax.ShapeDtypeStruct(shape, F32),
        in_specs=[pl.BlockSpec(memory_space=pltpu.SMEM)] + [spec] * (aliased + len(pieces)),
        out_specs=spec,
        scratch_shapes=[pltpu.SemaphoreType.DMA((len(pieces),))],
        input_output_aliases={1: 0} if aliased else {},
        compiler_params=pltpu.CompilerParams(vmem_limit_bytes=1 << 20),
        cost_estimate=pl.CostEstimate(flops=PUT_FLOPS, bytes_accessed=0, transcendentals=0),
        name="put",
    )(starts, *([weights] if aliased else []), *pieces)


def hidden_kernel(sizes, at, gate, up, mine, send):
    experts, length, own = sizes
    cap_rows = gate.shape[0] // experts
    at_e, core = at[0], at[1]
    values = []
    for j in range(experts):
        spot = pl.ds(pl.multiple_of(lax.rem(at_e + j, experts) * cap_rows, cap_rows), cap_rows)
        value = gate[spot, :].astype(F32)
        values.append(value / (1.0 + jnp.exp(-value)) * up[spot, :].astype(F32))
    value = jnp.concatenate(values, axis=0).T.astype(BF16)
    for chip in range(length):
        d = at[2 + chip]
        first = chip * 2 * own
        low, high = value[first : first + own], value[first + own : first + 2 * own]
        mine[d] = jnp.where(core == 0, low, high)
        send[d] = jnp.where(core == 0, high, low)


def hidden_pieces(at, gate, up, sizes):
    experts, length, own = sizes
    shape = jax.ShapeDtypeStruct((length, own, gate.shape[0]), BF16)
    vmem = pl.BlockSpec(memory_space=pltpu.VMEM)
    return pl.pallas_call(
        functools.partial(hidden_kernel, sizes),
        out_shape=(shape, shape),
        in_specs=[pl.BlockSpec(memory_space=pltpu.SMEM), vmem, vmem],
        out_specs=(vmem, vmem),
        compiler_params=pltpu.CompilerParams(vmem_limit_bytes=(8 << 20) * max(1, experts // 2)),
        cost_estimate=pl.CostEstimate(flops=HIDDEN_FLOPS, bytes_accessed=0, transcendentals=0),
        name="hidden_pieces",
    )(at, gate, up)


def product_kernel(scale, left, *refs):
    pieces, out, rows = refs[:-2], refs[-2], refs[-1]
    height = pieces[0].shape[0]
    for n, piece in enumerate(pieces):
        rows[n * height : (n + 1) * height, :] = piece[...]
    total = jnp.dot(left[...], rows[...], preferred_element_type=F32)
    out[...] = total * scale if scale != 1.0 else total


def product(left, pieces, scale):
    height, depth = left.shape
    size = pieces[0].shape[1]
    vmem = pl.BlockSpec(memory_space=pltpu.VMEM)
    return pl.pallas_call(
        functools.partial(product_kernel, scale),
        out_shape=jax.ShapeDtypeStruct((height, size), F32),
        in_specs=[vmem] * (1 + len(pieces)),
        out_specs=vmem,
        scratch_shapes=[pltpu.VMEM((depth, size), BF16)],
        compiler_params=pltpu.CompilerParams(vmem_limit_bytes=16 << 20),
        cost_estimate=pl.CostEstimate(flops=0, bytes_accessed=0, transcendentals=0),
        name="product",
    )(left, *pieces)


def build(mesh):
    devices = mesh.shape["dp"]
    experts = mesh.shape["expert"]
    rows_a = 4
    rows_b = devices // (2 * rows_a)

    def place(a, b, c):
        return ((a % rows_a) * rows_b + b % rows_b) * 2 + c % 2

    spots = [(a, b, c) for a in range(rows_a) for b in range(rows_b) for c in range(2)]

    ring = [(a, 0) for a in range(rows_a)]
    for n, a in enumerate(reversed(range(rows_a))):
        ring += [(a, b) for b in (range(1, rows_b) if n % 2 == 0 else reversed(range(1, rows_b)))]
    length = len(ring)
    sources = [[0] * length for _ in ring]
    distances = [[0] * length for _ in ring]
    for p, (a, b) in enumerate(ring):
        for d in range(length):
            from_a, from_b = ring[(p - d) % length]
            sources[a * rows_b + b][d] = from_a * rows_b + from_b
            distances[a * rows_b + b][from_a * rows_b + from_b] = (length - d) % length

    def step_ring(value, way):
        pairs = [(ring[p], ring[(p + way) % length]) for p in range(length)]
        return lax.ppermute(value, "dp", [(place(*x, c), place(*y, c)) for x, y in pairs for c in range(2)])

    def swap_core(value):
        return lax.ppermute(value, "dp", [(place(a, b, c), place(a, b, c + 1)) for a, b, c in spots])

    def shift_expert(value, k):
        return lax.ppermute(value, "expert", [(e, (e + k) % experts) for e in range(experts)])

    def local(grad_out, expert_ids, gate_probs, saved_gate, saved_up, master, moment_one, moment_two):
        me = lax.axis_index("dp")
        core = me % 2
        at_b = (me // 2) % rows_b
        at_a = me // (2 * rows_b)
        at_e = lax.axis_index("expert")
        tok_rows, dim = grad_out.shape
        cap_rows = tok_rows * 3 // 8
        own = master.shape[1]
        slot_rows, _, width = saved_gate.shape

        count = len(CHUNKS)
        cuts = [sum(CHUNKS[:i]) for i in range(count)]
        parts = dispatch(expert_ids, gate_probs, grad_out, cap_rows)

        chip = lax.dynamic_index_in_dim(jnp.array(sources, jnp.int32), me // 2, 0, False)
        ahead = lax.dynamic_index_in_dim(jnp.array(distances, jnp.int32), me // 2, 0, False)
        at = jnp.concatenate([jnp.stack([at_e, core]).astype(jnp.int32), ahead])
        hidden_mine, hidden_send = hidden_pieces(
            after(at, parts[0]),
            saved_gate.reshape(slot_rows, width),
            saved_up.reshape(slot_rows, width),
            (experts, length, own),
        )
        left = jnp.concatenate([hidden_mine, swap_core(hidden_send)], axis=2)
        left = left.reshape(length * own, 2 * slot_rows)

        largest = length // 2 * 2 * slot_rows * 36.0 * 0.2
        shrink = 1.0
        while largest * shrink > 60000.0:
            shrink *= 0.5

        middle = length // 2
        events = sorted((step + OFFSET * i, -i, i, step) for i in range(count) for step in range(middle))
        far, totals, moving = [], [], []
        token = hidden_mine
        for _, _, i, step in events:
            size = CHUNKS[i]
            cut = size // 2
            if step == 0:
                while len(far) < min(i + 2, count):
                    n = len(far)
                    part = parts[n] if n == 0 else after(parts[n], far[n - 1][-1])
                    far.append([shift_expert(part, -j) for j in range(1, experts)])
                here = [parts[i]] + [after(x, token) for x in far[i]]
                total = product(left, here + [swap_core(x) for x in here], shrink).reshape(length, own, size)
                totals.append(total)
                one, two = total[middle, :, :cut], total[middle, :, cut:]
                moving.append(None)
            else:
                total, d = totals[i], middle - step
                up, down = after(moving[i], token)
                one, two = total[d], total[length - d]
                if step == 1:
                    one = jnp.concatenate([one[:, :cut] + up.astype(F32), one[:, cut:]], axis=1)
                    two = jnp.concatenate([two[:, :cut], two[:, cut:] + down.astype(F32)], axis=1)
                else:
                    one, two = one + up.astype(F32), two + down.astype(F32)
            one, two = one.astype(F16), two.astype(F16)
            token = (one, two)
            moving[i] = (step_ring(one, 1), step_ring(two, -1))
        grads = [
            total[0] + up.astype(F32) + down.astype(F32)
            for total, (up, down) in ((totals[i], after(moving[i], token)) for i in range(count))
        ]
        grad = (jnp.concatenate(grads, axis=1) * (1.0 / shrink)).reshape(master.shape)

        new_one = 0.9 * moment_one + 0.1 * grad
        new_two = 0.95 * moment_two + 0.05 * grad * grad
        step = new_one / (1.0 - 0.9**20) / (jnp.sqrt(new_two / (1.0 - 0.95**20)) + 1e-08)
        wrms = jnp.sqrt(jnp.mean(master * master, axis=-1, keepdims=True) + 1e-06)
        srms = jnp.sqrt(jnp.mean(step * step, axis=-1, keepdims=True) + 1e-06)
        factor = jnp.minimum(1.0, 0.02 * wrms / (0.01 * srms))
        new_master = master - 0.01 * factor * step

        bound = jnp.max(jnp.abs(after(master[0], token)), axis=-1, keepdims=True) + 0.08
        power = jnp.floor(jnp.log2(bound))
        coded = (new_master[0] * jnp.exp2(13.0 - power)).astype(F16)
        coded = jnp.concatenate([coded, jnp.broadcast_to(power.astype(F16), (own, 128))], axis=1)
        steps = [[(0, 0, coded)]]
        ahead, back = coded, coded
        for i in range(1, length // 2):
            ahead, back = step_ring(ahead, 1), step_ring(back, -1)
            steps.append([(i, 0, ahead), (length - i, 0, back)])
        cut = dim // 2
        opposite = [step_ring(back[:, cut:], -1), step_ring(ahead[:, :cut], 1)]
        steps.append([(length // 2, cut, opposite[0]), (length // 2, 0, opposite[1])])
        starts = ((chip[:, None] * 2 + (core + jnp.arange(2, dtype=jnp.int32)) % 2) * own).astype(jnp.int32).reshape(-1)
        scales, weights, late = {}, None, []
        for step in steps[:-1] + [[]] + steps[-1:] + [[]]:
            pieces = late
            late = []
            for d, first, value in step:
                pieces = pieces + [((d, 0), first, value)]
                late.append(((d, 1), first, swap_core(value)))
            marks, values = [], []
            for spot, first, value in pieces:
                if first + value.shape[1] > dim:
                    scales[spot] = jnp.exp2(value[:, -1:].astype(F32) - 13.0)
                    value = value[:, : dim - first]
                values.append(value.astype(F32) * scales[spot])
                marks.append((spot[0] * 2 + spot[1], first))
            weights = put(weights, (width, dim), starts, marks, values)
        return (new_master, new_one, new_two, weights[None])

    return local


def solution(mesh):
    return jax.shard_map(
        build(mesh),
        mesh=mesh,
        in_specs=(
            P(("dp", "expert"), None),
            P(("dp", "expert"), None),
            P(("dp", "expert"), None),
            P("dp", "expert", None),
            P("dp", "expert", None),
            P("expert", "dp", None),
            P("expert", "dp", None),
            P("expert", "dp", None),
        ),
        out_specs=(
            P("expert", "dp", None),
            P("expert", "dp", None),
            P("expert", "dp", None),
            P("expert", None, None),
        ),
        check_vma=False,
    )
```

```python
import functools

import jax
import jax.numpy as jnp
from jax import lax
from jax.experimental import pallas as pl
from jax.experimental.pallas import tpu as pltpu
from jax.sharding import PartitionSpec as P

F16 = jnp.float16
F32 = jnp.float32
BF16 = jnp.bfloat16
CHUNKS = (1536, 1536)
PUT_FLOPS = 4 << 30
SPLIT = 1
HIDDEN_FLOPS = 8 << 30
OFFSET = 3
DISPATCH_FLOPS = 4 << 30
DISPATCH_VMEM = 56


def after(value, other):
    return lax.optimization_barrier((value, other))[0]


def dispatch_kernel(first, ids_in, probs_in, grad_in, out, ids, probs, grad, sems):
    cap_rows, size = out.shape
    cuts = [n * (size // 2) for n in range(2)]
    spots = [pl.ds(cut, size // 2) for cut in cuts]
    copies = [pltpu.make_async_copy(ids_in, ids, sems.at[0]), pltpu.make_async_copy(probs_in, probs, sems.at[1])]
    copies += [
        pltpu.make_async_copy(grad_in.at[:, pl.ds(first + cut, size // 2)], grad.at[:, spot], sems.at[2 + n])
        for n, (cut, spot) in enumerate(zip(cuts, spots))
    ]
    for copy in copies:
        copy.start()
    copies[0].wait()
    copies[1].wait()
    tok_rows = ids.shape[1]
    hit = ids[...] == 0
    weight = jnp.sum(jnp.where(hit, probs[...], 0.0), axis=0, keepdims=True)
    chosen = jnp.sum(jnp.where(hit, 1.0, 0.0), axis=0, keepdims=True)
    earlier = lax.broadcasted_iota(jnp.int32, (tok_rows, tok_rows), 0) < lax.broadcasted_iota(
        jnp.int32, (tok_rows, tok_rows), 1
    )
    slot = jnp.dot(
        jnp.broadcast_to(chosen, (8, tok_rows)).astype(BF16),
        jnp.where(earlier, 1.0, 0.0).astype(BF16),
        preferred_element_type=F32,
    )[:1]
    slot = jnp.where(chosen > 0.0, slot, -1.0)
    places = lax.broadcasted_iota(jnp.int32, (cap_rows, tok_rows), 0).astype(F32)
    placing = jnp.where(slot == places, 1.0, 0.0).astype(BF16)
    weight = jnp.broadcast_to(weight, (128, tok_rows)).T[:, :1]
    for n, spot in enumerate(spots):
        copies[2 + n].wait()
        scaled = (weight * grad[:, spot].astype(F32)).astype(BF16)
        out[:, spot] = jnp.dot(placing, scaled, preferred_element_type=F32).astype(BF16)


def dispatch(ids, probs, grad, cap_rows, first, size):
    vmem, hbm = pl.BlockSpec(memory_space=pltpu.VMEM), pl.BlockSpec(memory_space=pl.ANY)
    return pl.pallas_call(
        functools.partial(dispatch_kernel, first),
        out_shape=jax.ShapeDtypeStruct((cap_rows, size), BF16),
        in_specs=[hbm] * 3,
        out_specs=vmem,
        scratch_shapes=[
            pltpu.VMEM(ids.shape, ids.dtype),
            pltpu.VMEM(probs.shape, probs.dtype),
            pltpu.VMEM((grad.shape[0], size), grad.dtype),
            pltpu.SemaphoreType.DMA((4,)),
        ],
        compiler_params=pltpu.CompilerParams(vmem_limit_bytes=DISPATCH_VMEM << 20),
        cost_estimate=pl.CostEstimate(flops=DISPATCH_FLOPS, bytes_accessed=0, transcendentals=0),
        name="dispatch",
    )(ids, probs, grad)


def put_kernel(marks, aliased, starts, *refs):
    refs = refs[1:] if aliased else refs
    pieces, out, sems = refs[: len(marks)], refs[len(marks)], refs[len(marks) + 1]
    copies = []
    for n, (index, column) in enumerate(marks):
        height, size = pieces[n].shape
        part = height // SPLIT
        for k in range(SPLIT):
            row = pl.multiple_of(starts[index] + k * part, part)
            spot = out.at[pl.ds(row, part), pl.ds(column, size)]
            copies.append(
                pltpu.make_async_copy(pieces[n].at[pl.ds(k * part, part), :], spot, sems.at[n * SPLIT + k])
            )
            copies[-1].start()
    for copy in copies:
        copy.wait()


def put(weights, shape, starts, marks, pieces):
    aliased = weights is not None
    spec = pl.BlockSpec(memory_space=pl.ANY)
    return pl.pallas_call(
        functools.partial(put_kernel, tuple(marks), aliased),
        out_shape=jax.ShapeDtypeStruct(shape, F32),
        in_specs=[pl.BlockSpec(memory_space=pltpu.SMEM)] + [spec] * (aliased + len(pieces)),
        out_specs=spec,
        scratch_shapes=[pltpu.SemaphoreType.DMA((len(pieces) * SPLIT,))],
        input_output_aliases={1: 0} if aliased else {},
        compiler_params=pltpu.CompilerParams(vmem_limit_bytes=1 << 20),
        cost_estimate=pl.CostEstimate(flops=PUT_FLOPS, bytes_accessed=0, transcendentals=0),
        name="put",
    )(starts, *([weights] if aliased else []), *pieces)


def hidden_kernel(sizes, at, gate, up, mine, send):
    experts, length, own = sizes
    cap_rows = gate.shape[0] // experts
    at_e, core = at[0], at[1]
    values = []
    for j in range(experts):
        spot = pl.ds(pl.multiple_of(lax.rem(at_e + j, experts) * cap_rows, cap_rows), cap_rows)
        value = gate[spot, :].astype(F32)
        values.append(value / (1.0 + jnp.exp(-value)) * up[spot, :].astype(F32))
    value = jnp.concatenate(values, axis=0).T.astype(BF16)
    for chip in range(length):
        d = at[2 + chip]
        first = chip * 2 * own
        low, high = value[first : first + own], value[first + own : first + 2 * own]
        mine[d] = jnp.where(core == 0, low, high)
        send[d] = jnp.where(core == 0, high, low)


def hidden_pieces(at, gate, up, sizes):
    experts, length, own = sizes
    shape = jax.ShapeDtypeStruct((length, own, gate.shape[0]), BF16)
    vmem = pl.BlockSpec(memory_space=pltpu.VMEM)
    return pl.pallas_call(
        functools.partial(hidden_kernel, sizes),
        out_shape=(shape, shape),
        in_specs=[pl.BlockSpec(memory_space=pltpu.SMEM), vmem, vmem],
        out_specs=(vmem, vmem),
        compiler_params=pltpu.CompilerParams(vmem_limit_bytes=(8 << 20) * max(1, experts // 2)),
        cost_estimate=pl.CostEstimate(flops=HIDDEN_FLOPS, bytes_accessed=0, transcendentals=0),
        name="hidden_pieces",
    )(at, gate, up)


def product_kernel(scale, left, *refs):
    pieces, out, rows = refs[:-2], refs[-2], refs[-1]
    height = pieces[0].shape[0]
    for n, piece in enumerate(pieces):
        rows[n * height : (n + 1) * height, :] = piece[...]
    total = jnp.dot(left[...], rows[...], preferred_element_type=F32)
    out[...] = total * scale if scale != 1.0 else total


def product(left, pieces, scale):
    height, depth = left.shape
    size = pieces[0].shape[1]
    vmem = pl.BlockSpec(memory_space=pltpu.VMEM)
    return pl.pallas_call(
        functools.partial(product_kernel, scale),
        out_shape=jax.ShapeDtypeStruct((height, size), F32),
        in_specs=[vmem] * (1 + len(pieces)),
        out_specs=vmem,
        scratch_shapes=[pltpu.VMEM((depth, size), BF16)],
        compiler_params=pltpu.CompilerParams(vmem_limit_bytes=16 << 20),
        cost_estimate=pl.CostEstimate(flops=0, bytes_accessed=0, transcendentals=0),
        name="product",
    )(left, *pieces)


def build(mesh):
    devices = mesh.shape["dp"]
    experts = mesh.shape["expert"]
    rows_a = 4
    rows_b = devices // (2 * rows_a)

    def place(a, b, c):
        return ((a % rows_a) * rows_b + b % rows_b) * 2 + c % 2

    spots = [(a, b, c) for a in range(rows_a) for b in range(rows_b) for c in range(2)]

    ring = [(a, 0) for a in range(rows_a)]
    for n, a in enumerate(reversed(range(rows_a))):
        ring += [(a, b) for b in (range(1, rows_b) if n % 2 == 0 else reversed(range(1, rows_b)))]
    length = len(ring)
    sources = [[0] * length for _ in ring]
    distances = [[0] * length for _ in ring]
    for p, (a, b) in enumerate(ring):
        for d in range(length):
            from_a, from_b = ring[(p - d) % length]
            sources[a * rows_b + b][d] = from_a * rows_b + from_b
            distances[a * rows_b + b][from_a * rows_b + from_b] = (length - d) % length

    def step_ring(value, way):
        pairs = [(ring[p], ring[(p + way) % length]) for p in range(length)]
        return lax.ppermute(value, "dp", [(place(*x, c), place(*y, c)) for x, y in pairs for c in range(2)])

    def swap_core(value):
        return lax.ppermute(value, "dp", [(place(a, b, c), place(a, b, c + 1)) for a, b, c in spots])

    def shift_expert(value, k):
        return lax.ppermute(value, "expert", [(e, (e + k) % experts) for e in range(experts)])

    def local(grad_out, expert_ids, gate_probs, saved_gate, saved_up, master, moment_one, moment_two):
        me = lax.axis_index("dp")
        core = me % 2
        at_b = (me // 2) % rows_b
        at_a = me // (2 * rows_b)
        at_e = lax.axis_index("expert")
        tok_rows, dim = grad_out.shape
        cap_rows = tok_rows * 3 // 8
        own = master.shape[1]
        slot_rows, _, width = saved_gate.shape

        count = len(CHUNKS)
        cuts = [sum(CHUNKS[:i]) for i in range(count)]
        ids, probs = expert_ids.T, gate_probs.T
        parts = []
        for first, size in zip(cuts, CHUNKS):
            parts.append(dispatch(after(ids, parts[-1]) if parts else ids, probs, grad_out, cap_rows, first, size))

        chip = lax.dynamic_index_in_dim(jnp.array(sources, jnp.int32), me // 2, 0, False)
        ahead = lax.dynamic_index_in_dim(jnp.array(distances, jnp.int32), me // 2, 0, False)
        at = jnp.concatenate([jnp.stack([at_e, core]).astype(jnp.int32), ahead])
        hidden_mine, hidden_send = hidden_pieces(
            after(at, parts[0]),
            saved_gate.reshape(slot_rows, width),
            saved_up.reshape(slot_rows, width),
            (experts, length, own),
        )
        left = jnp.concatenate([hidden_mine, swap_core(hidden_send)], axis=2)
        left = left.reshape(length * own, 2 * slot_rows)

        largest = length // 2 * 2 * slot_rows * 36.0 * 0.2
        shrink = 1.0
        while largest * shrink > 60000.0:
            shrink *= 0.5

        middle = length // 2
        events = sorted((step + OFFSET * i, -i, i, step) for i in range(count) for step in range(middle))
        far, totals, moving = [], [], []
        token = (left, parts[-1])
        for _, _, i, step in events:
            size = CHUNKS[i]
            cut = size // 2
            if step == 0:
                while len(far) < min(i + 2, count):
                    n = len(far)
                    part = parts[n] if n == 0 else after(parts[n], far[n - 1][-1])
                    far.append([shift_expert(part, -j) for j in range(1, experts)])
                here = [parts[i]] + [after(x, token) for x in far[i]]
                total = product(left, here + [swap_core(x) for x in here], shrink).reshape(length, own, size)
                totals.append(total)
                one, two = total[middle, :, :cut], total[middle, :, cut:]
                moving.append(None)
            else:
                total, d = totals[i], middle - step
                up, down = after(moving[i], (token, far[i + 1]) if step == 2 and i + 1 < count else token)
                one, two = total[d], total[length - d]
                if step == 1:
                    one = jnp.concatenate([one[:, :cut] + up.astype(F32), one[:, cut:]], axis=1)
                    two = jnp.concatenate([two[:, :cut], two[:, cut:] + down.astype(F32)], axis=1)
                else:
                    one, two = one + up.astype(F32), two + down.astype(F32)
            one, two = one.astype(F16), two.astype(F16)
            token = (one, two)
            moving[i] = (step_ring(one, 1), step_ring(two, -1))
        grads = [
            total[0] + up.astype(F32) + down.astype(F32)
            for total, (up, down) in ((totals[i], after(moving[i], token)) for i in range(count))
        ]
        grad = (jnp.concatenate(grads, axis=1) * (1.0 / shrink)).reshape(master.shape)

        new_one = 0.9 * moment_one + 0.1 * grad
        new_two = 0.95 * moment_two + 0.05 * grad * grad
        step = new_one / (1.0 - 0.9**20) / (jnp.sqrt(new_two / (1.0 - 0.95**20)) + 1e-08)
        wrms = jnp.sqrt(jnp.mean(master * master, axis=-1, keepdims=True) + 1e-06)
        srms = jnp.sqrt(jnp.mean(step * step, axis=-1, keepdims=True) + 1e-06)
        factor = jnp.minimum(1.0, 0.02 * wrms / (0.01 * srms))
        new_master = master - 0.01 * factor * step

        bound = jnp.max(jnp.abs(after(master[0], token)), axis=-1, keepdims=True) + 0.08
        power = jnp.floor(jnp.log2(bound))
        coded = (new_master[0] * jnp.exp2(13.0 - power)).astype(F16)
        coded = jnp.concatenate([coded, jnp.broadcast_to(power.astype(F16), (own, 128))], axis=1)
        steps = [[(0, 0, coded)]]
        ahead, back = coded, coded
        for i in range(1, length // 2):
            ahead, back = step_ring(ahead, 1), step_ring(back, -1)
            steps.append([(i, 0, ahead), (length - i, 0, back)])
        cut = dim // 2
        opposite = [step_ring(back[:, cut:], -1), step_ring(ahead[:, :cut], 1)]
        steps.append([(length // 2, cut, opposite[0]), (length // 2, 0, opposite[1])])
        starts = ((chip[:, None] * 2 + (core + jnp.arange(2, dtype=jnp.int32)) % 2) * own).astype(jnp.int32).reshape(-1)
        scales, weights, late = {}, None, []
        for step in steps + [[]]:
            pieces = late
            late = []
            for d, first, value in step:
                pieces = pieces + [((d, 0), first, value)]
                late.append(((d, 1), first, swap_core(value)))
            marks, values = [], []
            for spot, first, value in pieces:
                if first + value.shape[1] > dim:
                    scales[spot] = jnp.exp2(value[:, -1:].astype(F32) - 13.0)
                    value = value[:, : dim - first]
                values.append(value.astype(F32) * scales[spot])
                marks.append((spot[0] * 2 + spot[1], first))
            weights = put(weights, (width, dim), starts, marks, values)
        return (new_master, new_one, new_two, weights[None])

    return local


def solution(mesh):
    return jax.shard_map(
        build(mesh),
        mesh=mesh,
        in_specs=(
            P(("dp", "expert"), None),
            P(("dp", "expert"), None),
            P(("dp", "expert"), None),
            P("dp", "expert", None),
            P("dp", "expert", None),
            P("expert", "dp", None),
            P("expert", "dp", None),
            P("expert", "dp", None),
        ),
        out_specs=(
            P("expert", "dp", None),
            P("expert", "dp", None),
            P("expert", "dp", None),
            P("expert", None, None),
        ),
        check_vma=False,
    )
```

```python
import functools

import jax
import jax.numpy as jnp
from jax import lax
from jax.experimental import pallas as pl
from jax.experimental.pallas import tpu as pltpu
from jax.sharding import PartitionSpec as P

F16 = jnp.float16
F32 = jnp.float32
BF16 = jnp.bfloat16
CHUNKS = (1536, 1536)
PUT_FLOPS = 4 << 30
SPLIT = 1
HIDDEN_FLOPS = 8 << 30
OFFSET = 3
FINE = 2
DISPATCH_FLOPS = 4 << 30
DISPATCH_VMEM = 56


def encode(value):
    largest = jnp.max(jnp.abs(value), axis=1, keepdims=True)
    power = jnp.floor(jnp.log2(jnp.maximum(largest, 1e-30)))
    root = jnp.sqrt(jnp.abs(value) * jnp.exp2(28.0 - power))
    code = jnp.where(value < 0.0, -root, root)
    tail = jnp.broadcast_to(power, (value.shape[0], 128))
    return jnp.round(jnp.concatenate([code, tail], axis=1)).astype(jnp.int16)


def decode(code):
    if code.dtype == F16:
        return code.astype(F32)
    root = code[:, :-128].astype(F32)
    return root * jnp.abs(root) * jnp.exp2(code[:, -1:].astype(F32) - 28.0)


def after(value, other):
    return lax.optimization_barrier((value, other))[0]


def dispatch_kernel(first, ids_in, probs_in, grad_in, out, ids, probs, grad, sems):
    cap_rows, size = out.shape
    cuts = [n * (size // 2) for n in range(2)]
    spots = [pl.ds(cut, size // 2) for cut in cuts]
    copies = [pltpu.make_async_copy(ids_in, ids, sems.at[0]), pltpu.make_async_copy(probs_in, probs, sems.at[1])]
    copies += [
        pltpu.make_async_copy(grad_in.at[:, pl.ds(first + cut, size // 2)], grad.at[:, spot], sems.at[2 + n])
        for n, (cut, spot) in enumerate(zip(cuts, spots))
    ]
    for copy in copies:
        copy.start()
    copies[0].wait()
    copies[1].wait()
    tok_rows = ids.shape[1]
    hit = ids[...] == 0
    weight = jnp.sum(jnp.where(hit, probs[...], 0.0), axis=0, keepdims=True)
    chosen = jnp.sum(jnp.where(hit, 1.0, 0.0), axis=0, keepdims=True)
    earlier = lax.broadcasted_iota(jnp.int32, (tok_rows, tok_rows), 0) < lax.broadcasted_iota(
        jnp.int32, (tok_rows, tok_rows), 1
    )
    slot = jnp.dot(
        jnp.broadcast_to(chosen, (8, tok_rows)).astype(BF16),
        jnp.where(earlier, 1.0, 0.0).astype(BF16),
        preferred_element_type=F32,
    )[:1]
    slot = jnp.where(chosen > 0.0, slot, -1.0)
    places = lax.broadcasted_iota(jnp.int32, (cap_rows, tok_rows), 0).astype(F32)
    placing = jnp.where(slot == places, 1.0, 0.0).astype(BF16)
    weight = jnp.broadcast_to(weight, (128, tok_rows)).T[:, :1]
    for n, spot in enumerate(spots):
        copies[2 + n].wait()
        scaled = (weight * grad[:, spot].astype(F32)).astype(BF16)
        out[:, spot] = jnp.dot(placing, scaled, preferred_element_type=F32).astype(BF16)


def dispatch(ids, probs, grad, cap_rows, first, size):
    vmem, hbm = pl.BlockSpec(memory_space=pltpu.VMEM), pl.BlockSpec(memory_space=pl.ANY)
    return pl.pallas_call(
        functools.partial(dispatch_kernel, first),
        out_shape=jax.ShapeDtypeStruct((cap_rows, size), BF16),
        in_specs=[hbm] * 3,
        out_specs=vmem,
        scratch_shapes=[
            pltpu.VMEM(ids.shape, ids.dtype),
            pltpu.VMEM(probs.shape, probs.dtype),
            pltpu.VMEM((grad.shape[0], size), grad.dtype),
            pltpu.SemaphoreType.DMA((4,)),
        ],
        compiler_params=pltpu.CompilerParams(vmem_limit_bytes=DISPATCH_VMEM << 20),
        cost_estimate=pl.CostEstimate(flops=DISPATCH_FLOPS, bytes_accessed=0, transcendentals=0),
        name="dispatch",
    )(ids, probs, grad)


def put_kernel(marks, aliased, starts, *refs):
    refs = refs[1:] if aliased else refs
    pieces, out, sems = refs[: len(marks)], refs[len(marks)], refs[len(marks) + 1]
    copies = []
    for n, (index, column) in enumerate(marks):
        height, size = pieces[n].shape
        part = height // SPLIT
        for k in range(SPLIT):
            row = pl.multiple_of(starts[index] + k * part, part)
            spot = out.at[pl.ds(row, part), pl.ds(column, size)]
            copies.append(
                pltpu.make_async_copy(pieces[n].at[pl.ds(k * part, part), :], spot, sems.at[n * SPLIT + k])
            )
            copies[-1].start()
    for copy in copies:
        copy.wait()


def put(weights, shape, starts, marks, pieces):
    aliased = weights is not None
    spec = pl.BlockSpec(memory_space=pl.ANY)
    return pl.pallas_call(
        functools.partial(put_kernel, tuple(marks), aliased),
        out_shape=jax.ShapeDtypeStruct(shape, F32),
        in_specs=[pl.BlockSpec(memory_space=pltpu.SMEM)] + [spec] * (aliased + len(pieces)),
        out_specs=spec,
        scratch_shapes=[pltpu.SemaphoreType.DMA((len(pieces) * SPLIT,))],
        input_output_aliases={1: 0} if aliased else {},
        compiler_params=pltpu.CompilerParams(vmem_limit_bytes=1 << 20),
        cost_estimate=pl.CostEstimate(flops=PUT_FLOPS, bytes_accessed=0, transcendentals=0),
        name="put",
    )(starts, *([weights] if aliased else []), *pieces)


def hidden_kernel(sizes, at, gate, up, mine, send):
    experts, length, own = sizes
    cap_rows = gate.shape[0] // experts
    at_e, core = at[0], at[1]
    values = []
    for j in range(experts):
        spot = pl.ds(pl.multiple_of(lax.rem(at_e + j, experts) * cap_rows, cap_rows), cap_rows)
        value = gate[spot, :].astype(F32)
        values.append(value / (1.0 + jnp.exp(-value)) * up[spot, :].astype(F32))
    value = jnp.concatenate(values, axis=0).T.astype(BF16)
    for chip in range(length):
        d = at[2 + chip]
        first = chip * 2 * own
        low, high = value[first : first + own], value[first + own : first + 2 * own]
        mine[d] = jnp.where(core == 0, low, high)
        send[d] = jnp.where(core == 0, high, low)


def hidden_pieces(at, gate, up, sizes):
    experts, length, own = sizes
    shape = jax.ShapeDtypeStruct((length, own, gate.shape[0]), BF16)
    vmem = pl.BlockSpec(memory_space=pltpu.VMEM)
    return pl.pallas_call(
        functools.partial(hidden_kernel, sizes),
        out_shape=(shape, shape),
        in_specs=[pl.BlockSpec(memory_space=pltpu.SMEM), vmem, vmem],
        out_specs=(vmem, vmem),
        compiler_params=pltpu.CompilerParams(vmem_limit_bytes=(8 << 20) * max(1, experts // 2)),
        cost_estimate=pl.CostEstimate(flops=HIDDEN_FLOPS, bytes_accessed=0, transcendentals=0),
        name="hidden_pieces",
    )(at, gate, up)


def product_kernel(scale, left, *refs):
    pieces, out, rows = refs[:-2], refs[-2], refs[-1]
    height = pieces[0].shape[0]
    for n, piece in enumerate(pieces):
        rows[n * height : (n + 1) * height, :] = piece[...]
    total = jnp.dot(left[...], rows[...], preferred_element_type=F32)
    out[...] = total * scale if scale != 1.0 else total


def product(left, pieces, scale):
    height, depth = left.shape
    size = pieces[0].shape[1]
    vmem = pl.BlockSpec(memory_space=pltpu.VMEM)
    return pl.pallas_call(
        functools.partial(product_kernel, scale),
        out_shape=jax.ShapeDtypeStruct((height, size), F32),
        in_specs=[vmem] * (1 + len(pieces)),
        out_specs=vmem,
        scratch_shapes=[pltpu.VMEM((depth, size), BF16)],
        compiler_params=pltpu.CompilerParams(vmem_limit_bytes=16 << 20),
        cost_estimate=pl.CostEstimate(flops=0, bytes_accessed=0, transcendentals=0),
        name="product",
    )(left, *pieces)


def build(mesh):
    devices = mesh.shape["dp"]
    experts = mesh.shape["expert"]
    rows_a = 4
    rows_b = devices // (2 * rows_a)

    def place(a, b, c):
        return ((a % rows_a) * rows_b + b % rows_b) * 2 + c % 2

    spots = [(a, b, c) for a in range(rows_a) for b in range(rows_b) for c in range(2)]

    ring = [(a, 0) for a in range(rows_a)]
    for n, a in enumerate(reversed(range(rows_a))):
        ring += [(a, b) for b in (range(1, rows_b) if n % 2 == 0 else reversed(range(1, rows_b)))]
    length = len(ring)
    sources = [[0] * length for _ in ring]
    distances = [[0] * length for _ in ring]
    for p, (a, b) in enumerate(ring):
        for d in range(length):
            from_a, from_b = ring[(p - d) % length]
            sources[a * rows_b + b][d] = from_a * rows_b + from_b
            distances[a * rows_b + b][from_a * rows_b + from_b] = (length - d) % length

    def step_ring(value, way):
        pairs = [(ring[p], ring[(p + way) % length]) for p in range(length)]
        return lax.ppermute(value, "dp", [(place(*x, c), place(*y, c)) for x, y in pairs for c in range(2)])

    def swap_core(value):
        return lax.ppermute(value, "dp", [(place(a, b, c), place(a, b, c + 1)) for a, b, c in spots])

    def shift_expert(value, k):
        return lax.ppermute(value, "expert", [(e, (e + k) % experts) for e in range(experts)])

    def local(grad_out, expert_ids, gate_probs, saved_gate, saved_up, master, moment_one, moment_two):
        me = lax.axis_index("dp")
        core = me % 2
        at_b = (me // 2) % rows_b
        at_a = me // (2 * rows_b)
        at_e = lax.axis_index("expert")
        tok_rows, dim = grad_out.shape
        cap_rows = tok_rows * 3 // 8
        own = master.shape[1]
        slot_rows, _, width = saved_gate.shape

        count = len(CHUNKS)
        cuts = [sum(CHUNKS[:i]) for i in range(count)]
        ids, probs = expert_ids.T, gate_probs.T
        parts = []
        for first, size in zip(cuts, CHUNKS):
            parts.append(dispatch(after(ids, parts[-1]) if parts else ids, probs, grad_out, cap_rows, first, size))

        chip = lax.dynamic_index_in_dim(jnp.array(sources, jnp.int32), me // 2, 0, False)
        ahead = lax.dynamic_index_in_dim(jnp.array(distances, jnp.int32), me // 2, 0, False)
        at = jnp.concatenate([jnp.stack([at_e, core]).astype(jnp.int32), ahead])
        hidden_mine, hidden_send = hidden_pieces(
            after(at, parts[0]),
            saved_gate.reshape(slot_rows, width),
            saved_up.reshape(slot_rows, width),
            (experts, length, own),
        )
        left = jnp.concatenate([hidden_mine, swap_core(hidden_send)], axis=2)
        left = left.reshape(length * own, 2 * slot_rows)

        largest = length // 2 * 2 * slot_rows * 36.0 * 0.2
        shrink = 1.0
        while largest * shrink > 60000.0:
            shrink *= 0.5

        middle = length // 2
        events = sorted((step + OFFSET * i, -i, i, step) for i in range(count) for step in range(middle))
        far, totals, moving = [], [], []
        token = (left, parts[-1])
        for _, _, i, step in events:
            size = CHUNKS[i]
            cut = size // 2
            if step == 0:
                while len(far) < min(i + 2, count):
                    n = len(far)
                    part = parts[n] if n == 0 else after(parts[n], far[n - 1][-1])
                    far.append([shift_expert(part, -j) for j in range(1, experts)])
                here = [parts[i]] + [after(x, token) for x in far[i]]
                total = product(left, here + [swap_core(x) for x in here], shrink).reshape(length, own, size)
                totals.append(total)
                one, two = total[middle, :, :cut], total[middle, :, cut:]
                moving.append(None)
            else:
                total, d = totals[i], middle - step
                up, down = after(moving[i], (token, far[i + 1]) if step == 2 and i + 1 < count else token)
                one, two = total[d], total[length - d]
                if step == 1:
                    one = jnp.concatenate([one[:, :cut] + decode(up), one[:, cut:]], axis=1)
                    two = jnp.concatenate([two[:, :cut], two[:, cut:] + decode(down)], axis=1)
                else:
                    one, two = one + decode(up), two + decode(down)
            pack = encode if step >= middle - FINE else (lambda x: x.astype(F16))
            one, two = pack(one), pack(two)
            token = (one, two)
            moving[i] = (step_ring(one, 1), step_ring(two, -1))
        grads = [
            total[0] + decode(up) + decode(down)
            for total, (up, down) in ((totals[i], after(moving[i], token)) for i in range(count))
        ]
        grad = (jnp.concatenate(grads, axis=1) * (1.0 / shrink)).reshape(master.shape)

        new_one = 0.9 * moment_one + 0.1 * grad
        new_two = 0.95 * moment_two + 0.05 * grad * grad
        step = new_one / (1.0 - 0.9**20) / (jnp.sqrt(new_two / (1.0 - 0.95**20)) + 1e-08)
        wrms = jnp.sqrt(jnp.mean(master * master, axis=-1, keepdims=True) + 1e-06)
        srms = jnp.sqrt(jnp.mean(step * step, axis=-1, keepdims=True) + 1e-06)
        factor = jnp.minimum(1.0, 0.02 * wrms / (0.01 * srms))
        new_master = master - 0.01 * factor * step

        bound = jnp.max(jnp.abs(after(master[0], token)), axis=-1, keepdims=True) + 0.08
        power = jnp.floor(jnp.log2(bound))
        coded = (new_master[0] * jnp.exp2(13.0 - power)).astype(F16)
        coded = jnp.concatenate([coded, jnp.broadcast_to(power.astype(F16), (own, 128))], axis=1)
        steps = [[(0, 0, coded)]]
        ahead, back = coded, coded
        for i in range(1, length // 2):
            ahead, back = step_ring(ahead, 1), step_ring(back, -1)
            steps.append([(i, 0, ahead), (length - i, 0, back)])
        cut = dim // 2
        opposite = [step_ring(back[:, cut:], -1), step_ring(ahead[:, :cut], 1)]
        steps.append([(length // 2, cut, opposite[0]), (length // 2, 0, opposite[1])])
        starts = ((chip[:, None] * 2 + (core + jnp.arange(2, dtype=jnp.int32)) % 2) * own).astype(jnp.int32).reshape(-1)
        scales, weights, late = {}, None, []
        for step in steps + [[]]:
            pieces = late
            late = []
            for d, first, value in step:
                pieces = pieces + [((d, 0), first, value)]
                late.append(((d, 1), first, swap_core(value)))
            marks, values = [], []
            for spot, first, value in pieces:
                if first + value.shape[1] > dim:
                    scales[spot] = jnp.exp2(value[:, -1:].astype(F32) - 13.0)
                    value = value[:, : dim - first]
                values.append(value.astype(F32) * scales[spot])
                marks.append((spot[0] * 2 + spot[1], first))
            weights = put(weights, (width, dim), starts, marks, values)
        return (new_master, new_one, new_two, weights[None])

    return local


def solution(mesh):
    return jax.shard_map(
        build(mesh),
        mesh=mesh,
        in_specs=(
            P(("dp", "expert"), None),
            P(("dp", "expert"), None),
            P(("dp", "expert"), None),
            P("dp", "expert", None),
            P("dp", "expert", None),
            P("expert", "dp", None),
            P("expert", "dp", None),
            P("expert", "dp", None),
        ),
        out_specs=(
            P("expert", "dp", None),
            P("expert", "dp", None),
            P("expert", "dp", None),
            P("expert", None, None),
        ),
        check_vma=False,
    )
```

```python
import functools

import jax
import jax.numpy as jnp
from jax import lax
from jax.experimental import pallas as pl
from jax.experimental.pallas import tpu as pltpu
from jax.sharding import PartitionSpec as P

F16 = jnp.float16
F32 = jnp.float32
BF16 = jnp.bfloat16
CHUNKS = (1536, 1536)
PUT_FLOPS = 4 << 30
SPLIT = 1
HIDDEN_FLOPS = 8 << 30
OFFSET = 3
FINE = 1
DISPATCH_FLOPS = 4 << 30
DISPATCH_VMEM = 56


def encode(value):
    largest = jnp.max(jnp.abs(value), axis=1, keepdims=True)
    power = jnp.floor(jnp.log2(jnp.maximum(largest, 1e-20)))
    root = jnp.sqrt(jnp.abs(value) * jnp.exp2(28.0 - power))
    code = jnp.where(value < 0.0, -root, root)
    tail = jnp.broadcast_to(power, (value.shape[0], 128))
    return jnp.round(jnp.concatenate([code, tail], axis=1)).astype(jnp.int16)


def decode(code):
    if code.dtype == F16:
        return code.astype(F32)
    root = code[:, :-128].astype(F32)
    return root * jnp.abs(root) * jnp.exp2(code[:, -1:].astype(F32) - 28.0)


def after(value, other):
    return lax.optimization_barrier((value, other))[0]


def dispatch_kernel(first, ids_in, probs_in, grad_in, out, ids, probs, grad, sems):
    cap_rows, size = out.shape
    cuts = [n * (size // 2) for n in range(2)]
    spots = [pl.ds(cut, size // 2) for cut in cuts]
    copies = [pltpu.make_async_copy(ids_in, ids, sems.at[0]), pltpu.make_async_copy(probs_in, probs, sems.at[1])]
    copies += [
        pltpu.make_async_copy(grad_in.at[:, pl.ds(first + cut, size // 2)], grad.at[:, spot], sems.at[2 + n])
        for n, (cut, spot) in enumerate(zip(cuts, spots))
    ]
    for copy in copies:
        copy.start()
    copies[0].wait()
    copies[1].wait()
    tok_rows = ids.shape[1]
    hit = ids[...] == 0
    weight = jnp.sum(jnp.where(hit, probs[...], 0.0), axis=0, keepdims=True)
    chosen = jnp.sum(jnp.where(hit, 1.0, 0.0), axis=0, keepdims=True)
    earlier = lax.broadcasted_iota(jnp.int32, (tok_rows, tok_rows), 0) < lax.broadcasted_iota(
        jnp.int32, (tok_rows, tok_rows), 1
    )
    slot = jnp.dot(
        jnp.broadcast_to(chosen, (8, tok_rows)).astype(BF16),
        jnp.where(earlier, 1.0, 0.0).astype(BF16),
        preferred_element_type=F32,
    )[:1]
    slot = jnp.where(chosen > 0.0, slot, -1.0)
    places = lax.broadcasted_iota(jnp.int32, (cap_rows, tok_rows), 0).astype(F32)
    placing = jnp.where(slot == places, 1.0, 0.0).astype(BF16)
    weight = jnp.broadcast_to(weight, (128, tok_rows)).T[:, :1]
    for n, spot in enumerate(spots):
        copies[2 + n].wait()
        scaled = (weight * grad[:, spot].astype(F32)).astype(BF16)
        out[:, spot] = jnp.dot(placing, scaled, preferred_element_type=F32).astype(BF16)


def dispatch(ids, probs, grad, cap_rows, first, size):
    vmem, hbm = pl.BlockSpec(memory_space=pltpu.VMEM), pl.BlockSpec(memory_space=pl.ANY)
    return pl.pallas_call(
        functools.partial(dispatch_kernel, first),
        out_shape=jax.ShapeDtypeStruct((cap_rows, size), BF16),
        in_specs=[hbm] * 3,
        out_specs=vmem,
        scratch_shapes=[
            pltpu.VMEM(ids.shape, ids.dtype),
            pltpu.VMEM(probs.shape, probs.dtype),
            pltpu.VMEM((grad.shape[0], size), grad.dtype),
            pltpu.SemaphoreType.DMA((4,)),
        ],
        compiler_params=pltpu.CompilerParams(vmem_limit_bytes=DISPATCH_VMEM << 20),
        cost_estimate=pl.CostEstimate(flops=DISPATCH_FLOPS, bytes_accessed=0, transcendentals=0),
        name="dispatch",
    )(ids, probs, grad)


def put_kernel(marks, aliased, starts, *refs):
    refs = refs[1:] if aliased else refs
    pieces, out, sems = refs[: len(marks)], refs[len(marks)], refs[len(marks) + 1]
    copies = []
    for n, (index, column) in enumerate(marks):
        height, size = pieces[n].shape
        part = height // SPLIT
        for k in range(SPLIT):
            row = pl.multiple_of(starts[index] + k * part, part)
            spot = out.at[pl.ds(row, part), pl.ds(column, size)]
            copies.append(
                pltpu.make_async_copy(pieces[n].at[pl.ds(k * part, part), :], spot, sems.at[n * SPLIT + k])
            )
            copies[-1].start()
    for copy in copies:
        copy.wait()


def put(weights, shape, starts, marks, pieces):
    aliased = weights is not None
    spec = pl.BlockSpec(memory_space=pl.ANY)
    return pl.pallas_call(
        functools.partial(put_kernel, tuple(marks), aliased),
        out_shape=jax.ShapeDtypeStruct(shape, F32),
        in_specs=[pl.BlockSpec(memory_space=pltpu.SMEM)] + [spec] * (aliased + len(pieces)),
        out_specs=spec,
        scratch_shapes=[pltpu.SemaphoreType.DMA((len(pieces) * SPLIT,))],
        input_output_aliases={1: 0} if aliased else {},
        compiler_params=pltpu.CompilerParams(vmem_limit_bytes=1 << 20),
        cost_estimate=pl.CostEstimate(flops=PUT_FLOPS, bytes_accessed=0, transcendentals=0),
        name="put",
    )(starts, *([weights] if aliased else []), *pieces)


def hidden_kernel(sizes, at, gate, up, mine, send):
    experts, length, own = sizes
    cap_rows = gate.shape[0] // experts
    at_e, core = at[0], at[1]
    values = []
    for j in range(experts):
        spot = pl.ds(pl.multiple_of(lax.rem(at_e + j, experts) * cap_rows, cap_rows), cap_rows)
        value = gate[spot, :].astype(F32)
        values.append(value / (1.0 + jnp.exp(-value)) * up[spot, :].astype(F32))
    value = jnp.concatenate(values, axis=0).T.astype(BF16)
    for chip in range(length):
        d = at[2 + chip]
        first = chip * 2 * own
        low, high = value[first : first + own], value[first + own : first + 2 * own]
        mine[d] = jnp.where(core == 0, low, high)
        send[d] = jnp.where(core == 0, high, low)


def hidden_pieces(at, gate, up, sizes):
    experts, length, own = sizes
    shape = jax.ShapeDtypeStruct((length, own, gate.shape[0]), BF16)
    vmem = pl.BlockSpec(memory_space=pltpu.VMEM)
    return pl.pallas_call(
        functools.partial(hidden_kernel, sizes),
        out_shape=(shape, shape),
        in_specs=[pl.BlockSpec(memory_space=pltpu.SMEM), vmem, vmem],
        out_specs=(vmem, vmem),
        compiler_params=pltpu.CompilerParams(vmem_limit_bytes=(8 << 20) * max(1, experts // 2)),
        cost_estimate=pl.CostEstimate(flops=HIDDEN_FLOPS, bytes_accessed=0, transcendentals=0),
        name="hidden_pieces",
    )(at, gate, up)


def product_kernel(scale, left, *refs):
    pieces, out, rows = refs[:-2], refs[-2], refs[-1]
    height = pieces[0].shape[0]
    for n, piece in enumerate(pieces):
        rows[n * height : (n + 1) * height, :] = piece[...]
    total = jnp.dot(left[...], rows[...], preferred_element_type=F32)
    out[...] = total * scale if scale != 1.0 else total


def product(left, pieces, scale):
    height, depth = left.shape
    size = pieces[0].shape[1]
    vmem = pl.BlockSpec(memory_space=pltpu.VMEM)
    return pl.pallas_call(
        functools.partial(product_kernel, scale),
        out_shape=jax.ShapeDtypeStruct((height, size), F32),
        in_specs=[vmem] * (1 + len(pieces)),
        out_specs=vmem,
        scratch_shapes=[pltpu.VMEM((depth, size), BF16)],
        compiler_params=pltpu.CompilerParams(vmem_limit_bytes=16 << 20),
        cost_estimate=pl.CostEstimate(flops=0, bytes_accessed=0, transcendentals=0),
        name="product",
    )(left, *pieces)


def build(mesh):
    devices = mesh.shape["dp"]
    experts = mesh.shape["expert"]
    rows_a = 4
    rows_b = devices // (2 * rows_a)

    def place(a, b, c):
        return ((a % rows_a) * rows_b + b % rows_b) * 2 + c % 2

    spots = [(a, b, c) for a in range(rows_a) for b in range(rows_b) for c in range(2)]

    ring = [(a, 0) for a in range(rows_a)]
    for n, a in enumerate(reversed(range(rows_a))):
        ring += [(a, b) for b in (range(1, rows_b) if n % 2 == 0 else reversed(range(1, rows_b)))]
    length = len(ring)
    sources = [[0] * length for _ in ring]
    distances = [[0] * length for _ in ring]
    for p, (a, b) in enumerate(ring):
        for d in range(length):
            from_a, from_b = ring[(p - d) % length]
            sources[a * rows_b + b][d] = from_a * rows_b + from_b
            distances[a * rows_b + b][from_a * rows_b + from_b] = (length - d) % length

    def step_ring(value, way):
        pairs = [(ring[p], ring[(p + way) % length]) for p in range(length)]
        return lax.ppermute(value, "dp", [(place(*x, c), place(*y, c)) for x, y in pairs for c in range(2)])

    def swap_core(value):
        return lax.ppermute(value, "dp", [(place(a, b, c), place(a, b, c + 1)) for a, b, c in spots])

    def shift_expert(value, k):
        return lax.ppermute(value, "expert", [(e, (e + k) % experts) for e in range(experts)])

    def local(grad_out, expert_ids, gate_probs, saved_gate, saved_up, master, moment_one, moment_two):
        me = lax.axis_index("dp")
        core = me % 2
        at_b = (me // 2) % rows_b
        at_a = me // (2 * rows_b)
        at_e = lax.axis_index("expert")
        tok_rows, dim = grad_out.shape
        cap_rows = tok_rows * 3 // 8
        own = master.shape[1]
        slot_rows, _, width = saved_gate.shape

        count = len(CHUNKS)
        cuts = [sum(CHUNKS[:i]) for i in range(count)]
        ids, probs = expert_ids.T, gate_probs.T
        parts = []
        for first, size in zip(cuts, CHUNKS):
            parts.append(dispatch(after(ids, parts[-1]) if parts else ids, probs, grad_out, cap_rows, first, size))

        chip = lax.dynamic_index_in_dim(jnp.array(sources, jnp.int32), me // 2, 0, False)
        ahead = lax.dynamic_index_in_dim(jnp.array(distances, jnp.int32), me // 2, 0, False)
        at = jnp.concatenate([jnp.stack([at_e, core]).astype(jnp.int32), ahead])
        hidden_mine, hidden_send = hidden_pieces(
            after(at, parts[0]),
            saved_gate.reshape(slot_rows, width),
            saved_up.reshape(slot_rows, width),
            (experts, length, own),
        )
        left = jnp.concatenate([hidden_mine, swap_core(hidden_send)], axis=2)
        left = left.reshape(length * own, 2 * slot_rows)

        largest = length // 2 * 2 * slot_rows * 36.0 * 0.2
        shrink = 1.0
        while largest * shrink > 60000.0:
            shrink *= 0.5

        middle = length // 2
        events = sorted((step + OFFSET * i, -i, i, step) for i in range(count) for step in range(middle))
        far, totals, moving = [], [], []
        token = (left, parts[-1])
        for _, _, i, step in events:
            size = CHUNKS[i]
            cut = size // 2
            if step == 0:
                while len(far) < min(i + 2, count):
                    n = len(far)
                    part = parts[n] if n == 0 else after(parts[n], far[n - 1][-1])
                    far.append([shift_expert(part, -j) for j in range(1, experts)])
                here = [parts[i]] + [after(x, token) for x in far[i]]
                total = product(left, here + [swap_core(x) for x in here], shrink).reshape(length, own, size)
                totals.append(total)
                one, two = total[middle, :, :cut], total[middle, :, cut:]
                moving.append(None)
            else:
                total, d = totals[i], middle - step
                up, down = after(moving[i], (token, far[i + 1]) if step == 2 and i + 1 < count else token)
                one, two = total[d], total[length - d]
                if step == 1:
                    one = jnp.concatenate([one[:, :cut] + decode(up), one[:, cut:]], axis=1)
                    two = jnp.concatenate([two[:, :cut], two[:, cut:] + decode(down)], axis=1)
                else:
                    one, two = one + decode(up), two + decode(down)
            pack = encode if step >= middle - FINE else (lambda x: x.astype(F16))
            one, two = pack(one), pack(two)
            token = (one, two)
            moving[i] = (step_ring(one, 1), step_ring(two, -1))
        grads = [
            total[0] + decode(up) + decode(down)
            for total, (up, down) in ((totals[i], after(moving[i], token)) for i in range(count))
        ]
        grad = (jnp.concatenate(grads, axis=1) * (1.0 / shrink)).reshape(master.shape)

        new_one = 0.9 * moment_one + 0.1 * grad
        new_two = 0.95 * moment_two + 0.05 * grad * grad
        step = new_one / (1.0 - 0.9**20) / (jnp.sqrt(new_two / (1.0 - 0.95**20)) + 1e-08)
        wrms = jnp.sqrt(jnp.mean(master * master, axis=-1, keepdims=True) + 1e-06)
        srms = jnp.sqrt(jnp.mean(step * step, axis=-1, keepdims=True) + 1e-06)
        factor = jnp.minimum(1.0, 0.02 * wrms / (0.01 * srms))
        new_master = master - 0.01 * factor * step

        bound = jnp.max(jnp.abs(after(master[0], token)), axis=-1, keepdims=True) + 0.08
        power = jnp.floor(jnp.log2(bound))
        coded = (new_master[0] * jnp.exp2(13.0 - power)).astype(F16)
        coded = jnp.concatenate([coded, jnp.broadcast_to(power.astype(F16), (own, 128))], axis=1)
        steps = [[(0, 0, coded)]]
        ahead, back = coded, coded
        for i in range(1, length // 2):
            ahead, back = step_ring(ahead, 1), step_ring(back, -1)
            steps.append([(i, 0, ahead), (length - i, 0, back)])
        cut = dim // 2
        opposite = [step_ring(back[:, cut:], -1), step_ring(ahead[:, :cut], 1)]
        steps.append([(length // 2, cut, opposite[0]), (length // 2, 0, opposite[1])])
        starts = ((chip[:, None] * 2 + (core + jnp.arange(2, dtype=jnp.int32)) % 2) * own).astype(jnp.int32).reshape(-1)
        scales, weights, late = {}, None, []
        for step in steps + [[]]:
            pieces = late
            late = []
            for d, first, value in step:
                pieces = pieces + [((d, 0), first, value)]
                late.append(((d, 1), first, swap_core(value)))
            marks, values = [], []
            for spot, first, value in pieces:
                if first + value.shape[1] > dim:
                    scales[spot] = jnp.exp2(value[:, -1:].astype(F32) - 13.0)
                    value = value[:, : dim - first]
                values.append(value.astype(F32) * scales[spot])
                marks.append((spot[0] * 2 + spot[1], first))
            weights = put(weights, (width, dim), starts, marks, values)
        return (new_master, new_one, new_two, weights[None])

    return local


def solution(mesh):
    return jax.shard_map(
        build(mesh),
        mesh=mesh,
        in_specs=(
            P(("dp", "expert"), None),
            P(("dp", "expert"), None),
            P(("dp", "expert"), None),
            P("dp", "expert", None),
            P("dp", "expert", None),
            P("expert", "dp", None),
            P("expert", "dp", None),
            P("expert", "dp", None),
        ),
        out_specs=(
            P("expert", "dp", None),
            P("expert", "dp", None),
            P("expert", "dp", None),
            P("expert", None, None),
        ),
        check_vma=False,
    )
```

```python
import functools

import jax
import jax.numpy as jnp
from jax import lax
from jax.experimental import pallas as pl
from jax.experimental.pallas import tpu as pltpu
from jax.sharding import PartitionSpec as P

F16 = jnp.float16
F32 = jnp.float32
BF16 = jnp.bfloat16
CHUNKS = (1536, 1536)
PUT_FLOPS = 4 << 30
SPLIT = 1
HIDDEN_FLOPS = 8 << 30
OFFSET = 3
FINE = 2
DISPATCH_FLOPS = 4 << 30
DISPATCH_VMEM = 56


def encode(value):
    largest = jnp.max(jnp.abs(value), axis=1, keepdims=True)
    power = jnp.floor(jnp.log2(jnp.maximum(largest, 1e-20)))
    root = jnp.sqrt(jnp.abs(value) * jnp.exp2(28.0 - power))
    code = jnp.where(value < 0.0, -root, root)
    tail = jnp.broadcast_to(power, (value.shape[0], 128))
    return jnp.round(jnp.concatenate([code, tail], axis=1)).astype(jnp.int16)


def decode(code):
    if code.dtype == F16:
        return code.astype(F32)
    root = code[:, :-128].astype(F32)
    return root * jnp.abs(root) * jnp.exp2(code[:, -1:].astype(F32) - 28.0)


def after(value, other):
    return lax.optimization_barrier((value, other))[0]


def dispatch_kernel(first, ids_in, probs_in, grad_in, out, ids, probs, grad, sems):
    cap_rows, size = out.shape
    cuts = [n * (size // 2) for n in range(2)]
    spots = [pl.ds(cut, size // 2) for cut in cuts]
    copies = [pltpu.make_async_copy(ids_in, ids, sems.at[0]), pltpu.make_async_copy(probs_in, probs, sems.at[1])]
    copies += [
        pltpu.make_async_copy(grad_in.at[:, pl.ds(first + cut, size // 2)], grad.at[:, spot], sems.at[2 + n])
        for n, (cut, spot) in enumerate(zip(cuts, spots))
    ]
    for copy in copies:
        copy.start()
    copies[0].wait()
    copies[1].wait()
    tok_rows = ids.shape[1]
    hit = ids[...] == 0
    weight = jnp.sum(jnp.where(hit, probs[...], 0.0), axis=0, keepdims=True)
    chosen = jnp.sum(jnp.where(hit, 1.0, 0.0), axis=0, keepdims=True)
    earlier = lax.broadcasted_iota(jnp.int32, (tok_rows, tok_rows), 0) < lax.broadcasted_iota(
        jnp.int32, (tok_rows, tok_rows), 1
    )
    slot = jnp.dot(
        jnp.broadcast_to(chosen, (8, tok_rows)).astype(BF16),
        jnp.where(earlier, 1.0, 0.0).astype(BF16),
        preferred_element_type=F32,
    )[:1]
    slot = jnp.where(chosen > 0.0, slot, -1.0)
    places = lax.broadcasted_iota(jnp.int32, (cap_rows, tok_rows), 0).astype(F32)
    placing = jnp.where(slot == places, 1.0, 0.0).astype(BF16)
    weight = jnp.broadcast_to(weight, (128, tok_rows)).T[:, :1]
    for n, spot in enumerate(spots):
        copies[2 + n].wait()
        scaled = (weight * grad[:, spot].astype(F32)).astype(BF16)
        out[:, spot] = jnp.dot(placing, scaled, preferred_element_type=F32).astype(BF16)


def dispatch(ids, probs, grad, cap_rows, first, size):
    vmem, hbm = pl.BlockSpec(memory_space=pltpu.VMEM), pl.BlockSpec(memory_space=pl.ANY)
    return pl.pallas_call(
        functools.partial(dispatch_kernel, first),
        out_shape=jax.ShapeDtypeStruct((cap_rows, size), BF16),
        in_specs=[hbm] * 3,
        out_specs=vmem,
        scratch_shapes=[
            pltpu.VMEM(ids.shape, ids.dtype),
            pltpu.VMEM(probs.shape, probs.dtype),
            pltpu.VMEM((grad.shape[0], size), grad.dtype),
            pltpu.SemaphoreType.DMA((4,)),
        ],
        compiler_params=pltpu.CompilerParams(vmem_limit_bytes=DISPATCH_VMEM << 20),
        cost_estimate=pl.CostEstimate(flops=DISPATCH_FLOPS, bytes_accessed=0, transcendentals=0),
        name="dispatch",
    )(ids, probs, grad)


def put_kernel(marks, aliased, starts, *refs):
    refs = refs[1:] if aliased else refs
    pieces, out, sems = refs[: len(marks)], refs[len(marks)], refs[len(marks) + 1]
    copies = []
    for n, (index, column) in enumerate(marks):
        height, size = pieces[n].shape
        part = height // SPLIT
        for k in range(SPLIT):
            row = pl.multiple_of(starts[index] + k * part, part)
            spot = out.at[pl.ds(row, part), pl.ds(column, size)]
            copies.append(
                pltpu.make_async_copy(pieces[n].at[pl.ds(k * part, part), :], spot, sems.at[n * SPLIT + k])
            )
            copies[-1].start()
    for copy in copies:
        copy.wait()


def put(weights, shape, starts, marks, pieces):
    aliased = weights is not None
    spec = pl.BlockSpec(memory_space=pl.ANY)
    return pl.pallas_call(
        functools.partial(put_kernel, tuple(marks), aliased),
        out_shape=jax.ShapeDtypeStruct(shape, F32),
        in_specs=[pl.BlockSpec(memory_space=pltpu.SMEM)] + [spec] * (aliased + len(pieces)),
        out_specs=spec,
        scratch_shapes=[pltpu.SemaphoreType.DMA((len(pieces) * SPLIT,))],
        input_output_aliases={1: 0} if aliased else {},
        compiler_params=pltpu.CompilerParams(vmem_limit_bytes=1 << 20),
        cost_estimate=pl.CostEstimate(flops=PUT_FLOPS, bytes_accessed=0, transcendentals=0),
        name="put",
    )(starts, *([weights] if aliased else []), *pieces)


def hidden_kernel(sizes, at, gate, up, mine, send):
    experts, length, own = sizes
    cap_rows = gate.shape[0] // experts
    at_e, core = at[0], at[1]
    values = []
    for j in range(experts):
        spot = pl.ds(pl.multiple_of(lax.rem(at_e + j, experts) * cap_rows, cap_rows), cap_rows)
        value = gate[spot, :].astype(F32)
        values.append(value / (1.0 + jnp.exp(-value)) * up[spot, :].astype(F32))
    value = jnp.concatenate(values, axis=0).T.astype(BF16)
    for chip in range(length):
        d = at[2 + chip]
        first = chip * 2 * own
        low, high = value[first : first + own], value[first + own : first + 2 * own]
        mine[d] = jnp.where(core == 0, low, high)
        send[d] = jnp.where(core == 0, high, low)


def hidden_pieces(at, gate, up, sizes):
    experts, length, own = sizes
    shape = jax.ShapeDtypeStruct((length, own, gate.shape[0]), BF16)
    vmem = pl.BlockSpec(memory_space=pltpu.VMEM)
    return pl.pallas_call(
        functools.partial(hidden_kernel, sizes),
        out_shape=(shape, shape),
        in_specs=[pl.BlockSpec(memory_space=pltpu.SMEM), vmem, vmem],
        out_specs=(vmem, vmem),
        compiler_params=pltpu.CompilerParams(vmem_limit_bytes=(8 << 20) * max(1, experts // 2)),
        cost_estimate=pl.CostEstimate(flops=HIDDEN_FLOPS, bytes_accessed=0, transcendentals=0),
        name="hidden_pieces",
    )(at, gate, up)


def product_kernel(scale, left, *refs):
    pieces, out, rows = refs[:-2], refs[-2], refs[-1]
    height = pieces[0].shape[0]
    for n, piece in enumerate(pieces):
        rows[n * height : (n + 1) * height, :] = piece[...]
    total = jnp.dot(left[...], rows[...], preferred_element_type=F32)
    out[...] = total * scale if scale != 1.0 else total


def product(left, pieces, scale):
    height, depth = left.shape
    size = pieces[0].shape[1]
    vmem = pl.BlockSpec(memory_space=pltpu.VMEM)
    return pl.pallas_call(
        functools.partial(product_kernel, scale),
        out_shape=jax.ShapeDtypeStruct((height, size), F32),
        in_specs=[vmem] * (1 + len(pieces)),
        out_specs=vmem,
        scratch_shapes=[pltpu.VMEM((depth, size), BF16)],
        compiler_params=pltpu.CompilerParams(vmem_limit_bytes=16 << 20),
        cost_estimate=pl.CostEstimate(flops=0, bytes_accessed=0, transcendentals=0),
        name="product",
    )(left, *pieces)


def build(mesh):
    devices = mesh.shape["dp"]
    experts = mesh.shape["expert"]
    rows_a = 4
    rows_b = devices // (2 * rows_a)

    def place(a, b, c):
        return ((a % rows_a) * rows_b + b % rows_b) * 2 + c % 2

    spots = [(a, b, c) for a in range(rows_a) for b in range(rows_b) for c in range(2)]

    ring = [(a, 0) for a in range(rows_a)]
    for n, a in enumerate(reversed(range(rows_a))):
        ring += [(a, b) for b in (range(1, rows_b) if n % 2 == 0 else reversed(range(1, rows_b)))]
    length = len(ring)
    sources = [[0] * length for _ in ring]
    distances = [[0] * length for _ in ring]
    for p, (a, b) in enumerate(ring):
        for d in range(length):
            from_a, from_b = ring[(p - d) % length]
            sources[a * rows_b + b][d] = from_a * rows_b + from_b
            distances[a * rows_b + b][from_a * rows_b + from_b] = (length - d) % length

    def step_ring(value, way):
        pairs = [(ring[p], ring[(p + way) % length]) for p in range(length)]
        return lax.ppermute(value, "dp", [(place(*x, c), place(*y, c)) for x, y in pairs for c in range(2)])

    def swap_core(value):
        return lax.ppermute(value, "dp", [(place(a, b, c), place(a, b, c + 1)) for a, b, c in spots])

    def shift_expert(value, k):
        return lax.ppermute(value, "expert", [(e, (e + k) % experts) for e in range(experts)])

    def local(grad_out, expert_ids, gate_probs, saved_gate, saved_up, master, moment_one, moment_two):
        me = lax.axis_index("dp")
        core = me % 2
        at_b = (me // 2) % rows_b
        at_a = me // (2 * rows_b)
        at_e = lax.axis_index("expert")
        tok_rows, dim = grad_out.shape
        cap_rows = tok_rows * 3 // 8
        own = master.shape[1]
        slot_rows, _, width = saved_gate.shape

        count = len(CHUNKS)
        cuts = [sum(CHUNKS[:i]) for i in range(count)]
        ids, probs = expert_ids.T, gate_probs.T
        parts = []
        for first, size in zip(cuts, CHUNKS):
            parts.append(dispatch(after(ids, parts[-1]) if parts else ids, probs, grad_out, cap_rows, first, size))

        chip = lax.dynamic_index_in_dim(jnp.array(sources, jnp.int32), me // 2, 0, False)
        ahead = lax.dynamic_index_in_dim(jnp.array(distances, jnp.int32), me // 2, 0, False)
        at = jnp.concatenate([jnp.stack([at_e, core]).astype(jnp.int32), ahead])
        hidden_mine, hidden_send = hidden_pieces(
            after(at, parts[0]),
            saved_gate.reshape(slot_rows, width),
            saved_up.reshape(slot_rows, width),
            (experts, length, own),
        )
        left = jnp.concatenate([hidden_mine, swap_core(hidden_send)], axis=2)
        left = left.reshape(length * own, 2 * slot_rows)

        largest = length // 2 * 2 * slot_rows * 36.0 * 0.2
        shrink = 1.0
        while largest * shrink > 60000.0:
            shrink *= 0.5

        middle = length // 2
        events = sorted((step + OFFSET * i, -i, i, step) for i in range(count) for step in range(middle))
        far, totals, moving = [], [], []
        token = (left, parts[-1])
        for _, _, i, step in events:
            size = CHUNKS[i]
            cut = size // 2
            if step == 0:
                while len(far) < min(i + 2, count):
                    n = len(far)
                    part = parts[n] if n == 0 else after(parts[n], far[n - 1][-1])
                    far.append([shift_expert(part, -j) for j in range(1, experts)])
                here = [parts[i]] + [after(x, token) for x in far[i]]
                total = product(left, here + [swap_core(x) for x in here], shrink).reshape(length, own, size)
                totals.append(total)
                one, two = total[middle, :, :cut], total[middle, :, cut:]
                moving.append(None)
            else:
                total, d = totals[i], middle - step
                up, down = after(moving[i], (token, far[i + 1]) if step == 2 and i + 1 < count else token)
                one, two = total[d], total[length - d]
                if step == 1:
                    one = jnp.concatenate([one[:, :cut] + decode(up), one[:, cut:]], axis=1)
                    two = jnp.concatenate([two[:, :cut], two[:, cut:] + decode(down)], axis=1)
                else:
                    one, two = one + decode(up), two + decode(down)
            pack = encode if step >= middle - FINE else (lambda x: x.astype(F16))
            one, two = pack(one), pack(two)
            token = (one, two)
            moving[i] = (step_ring(one, 1), step_ring(two, -1))
        grads = [
            total[0] + decode(up) + decode(down)
            for total, (up, down) in ((totals[i], after(moving[i], token)) for i in range(count))
        ]
        grad = (jnp.concatenate(grads, axis=1) * (1.0 / shrink)).reshape(master.shape)

        new_one = 0.9 * moment_one + 0.1 * grad
        new_two = 0.95 * moment_two + 0.05 * grad * grad
        step = new_one / (1.0 - 0.9**20) / (jnp.sqrt(new_two / (1.0 - 0.95**20)) + 1e-08)
        wrms = jnp.sqrt(jnp.mean(master * master, axis=-1, keepdims=True) + 1e-06)
        srms = jnp.sqrt(jnp.mean(step * step, axis=-1, keepdims=True) + 1e-06)
        factor = jnp.minimum(1.0, 0.02 * wrms / (0.01 * srms))
        new_master = master - 0.01 * factor * step

        bound = jnp.max(jnp.abs(after(master[0], token)), axis=-1, keepdims=True) + 0.08
        power = jnp.floor(jnp.log2(bound))
        coded = (new_master[0] * jnp.exp2(13.0 - power)).astype(F16)
        coded = jnp.concatenate([coded, jnp.broadcast_to(power.astype(F16), (own, 128))], axis=1)
        steps = [[(0, 0, coded)]]
        ahead, back = coded, coded
        for i in range(1, length // 2):
            ahead, back = step_ring(ahead, 1), step_ring(back, -1)
            steps.append([(i, 0, ahead), (length - i, 0, back)])
        cut = dim // 2
        opposite = [step_ring(back[:, cut:], -1), step_ring(ahead[:, :cut], 1)]
        steps.append([(length // 2, cut, opposite[0]), (length // 2, 0, opposite[1])])
        starts = ((chip[:, None] * 2 + (core + jnp.arange(2, dtype=jnp.int32)) % 2) * own).astype(jnp.int32).reshape(-1)
        scales, weights, late = {}, None, []
        for step in steps + [[]]:
            pieces = late
            late = []
            for d, first, value in step:
                pieces = pieces + [((d, 0), first, value)]
                late.append(((d, 1), first, swap_core(value)))
            marks, values = [], []
            for spot, first, value in pieces:
                if first + value.shape[1] > dim:
                    scales[spot] = jnp.exp2(value[:, -1:].astype(F32) - 13.0)
                    value = value[:, : dim - first]
                values.append(value.astype(F32) * scales[spot])
                marks.append((spot[0] * 2 + spot[1], first))
            weights = put(weights, (width, dim), starts, marks, values)
        return (new_master, new_one, new_two, weights[None])

    return local


def solution(mesh):
    return jax.shard_map(
        build(mesh),
        mesh=mesh,
        in_specs=(
            P(("dp", "expert"), None),
            P(("dp", "expert"), None),
            P(("dp", "expert"), None),
            P("dp", "expert", None),
            P("dp", "expert", None),
            P("expert", "dp", None),
            P("expert", "dp", None),
            P("expert", "dp", None),
        ),
        out_specs=(
            P("expert", "dp", None),
            P("expert", "dp", None),
            P("expert", "dp", None),
            P("expert", None, None),
        ),
        check_vma=False,
    )
```
